512 devices in a mesh: lat: 16 (over x, y_hi, core), lon: 32 (over z, y_lo).
Axes of the slice: x: 4, y: 8 (y_hi: 2, y_lo: 4; y = y_hi * 4 + y_lo), z: 8, core: 2. Of those that a mesh axis runs over, the one named last changes fastest.
Arguments:
- fields: bfloat16 [368, 1024, 256], P('lat', 'lon'), may hold values from -6 to 6
- conv_weight: bfloat16 [3, 3, 256, 256], replicated, may hold values from -0.21875 to 0.21875
- spectral_gain: float32 [512, 256], replicated, may hold values from 0.25 to 4
- support: int32 [368], P('lat'), may hold values from 1 to 24, as said below
Outputs:
- mixed: bfloat16 [368, 1024, 256], P('lat', 'lon')
The draws below stay inside these ranges and needn't reach their ends.
Inputs may be any that keep to these rules, and one draw needn't show every extreme that they name: support[i] is the longitude half-width, in cells, of cycle i's convolution support.
All inputs are finite; a program needn't handle non-finite values.
Results may differ from the reference program's by a relative error of at most 0.015.
Values may be sent and summed in bfloat16 or wider, within the bound.
A program may use at most 128 MiB of HBM per device.

```python
import math
import jax
import jax.numpy as jnp
from jax import lax

NLAT = 368
NLON = 1024
C = 256
M = 512
SMAX = 24
N_LAT = 16


def draw_support(key, part):
    key = jax.random.fold_in(key, 11)
    cycle_index = jnp.arange(NLAT, dtype=jnp.int32)
    pole_gap = jnp.minimum(cycle_index, NLAT - 1 - cycle_index)
    scale_cycles = max(NLAT // 16, 1)
    pole_width = 1 + SMAX * scale_cycles // (pole_gap + scale_cycles)
    jitter = jax.random.randint(key, (NLAT,), -2, 3)
    widths = jnp.clip(pole_width + jitter, 1, SMAX)
    widths = jnp.where(pole_gap == 0, SMAX, widths)
    widths = jnp.where(cycle_index == NLAT // 2, 1, widths)
    return widths.astype(jnp.int32)


def shard_levels(key, extent, split, low, top_value):
    factor_of, own = 1.0, jax.random.fold_in(key, 6)
    for position, parts in split:
        steps = jnp.exp(jax.random.uniform(jax.random.fold_in(own, position), (parts,), jnp.float32, low / len(split), top_value / len(split)))
        factor_of = factor_of * jnp.repeat(steps, extent[position] // parts).reshape([-1 if axis == position else 1 for axis in range(len(extent))])
    return factor_of


def bell_draw(rng, shape, scale, most, cuts=(), kind=jnp.bfloat16):
    loudness = shard_levels(rng, shape, cuts, -0.22, 0.18) if cuts else 1.0
    entries = jax.random.normal(rng, shape, jnp.float32) * scale * loudness
    return jnp.minimum(jnp.maximum(entries, -most), most).astype(kind)


def setup_inputs(seed: int = 0) -> dict:
    streams_of = jax.random.split(jax.random.key(seed), 5)
    fields = bell_draw(streams_of[0], (NLAT, NLON, C), 1.0, 6.0, ((0, 16), (1, 32)))
    conv_weight = bell_draw(streams_of[1], (3, 3, C, C), (3 * C) ** -0.5, 0.21875)
    spectral_gain = jnp.clip(jnp.exp(jax.random.uniform(streams_of[2], (M, C), jnp.float32, math.log(0.25), math.log(4.0))), 0.25, 4.0)
    support = draw_support(jax.random.fold_in(streams_of[4], 71), 0)
    return dict(fields=fields, conv_weight=conv_weight, spectral_gain=spectral_gain, support=support)


def band_weights(offset, half_width):
    span_len = (half_width + 1).astype(jnp.float32)
    distance = jnp.abs(offset).astype(jnp.float32)
    inside = jnp.abs(offset) <= half_width
    triangle = jnp.where(inside, (span_len - distance) / span_len, 0.0)
    hat_basis = triangle
    odd_basis = offset.astype(jnp.float32) * triangle / span_len
    box_basis = jnp.where(inside, 1.0, 0.0) / jnp.sqrt(2.0 * half_width.astype(jnp.float32) + 1.0)
    return jnp.stack([hat_basis, odd_basis, box_basis], axis=0).astype(jnp.bfloat16)

def legendre_table(orders, cosines, cycle_sines, degrees):
    order_real = orders.astype(jnp.float32)[:, None]
    log_start = 0.5 * jnp.log((2.0 * order_real + 1.0) / 2.0) + 0.5 * (lax.lgamma(2.0 * order_real + 1.0) - 2.0 * order_real * math.log(2.0) - 2.0 * lax.lgamma(order_real + 1.0)) + order_real * jnp.log(cycle_sines)[None, :]
    start_scale = jnp.minimum(log_start, 0.0)
    diagonal_start = jnp.exp(log_start - start_scale)
    shrink = 2.0 ** (-24)
    shrink_log = 24.0 * math.log(2.0)

    def recurrence(previous, degree):
        latest, before, log_scale = previous
        degree_real = degree.astype(jnp.float32)
        lower_gap = (degree - orders)[:, None]
        upper_sum = (degree + orders)[:, None]
        divisor = jnp.maximum((lower_gap * upper_sum).astype(jnp.float32), 1.0)
        rise_factor = jnp.sqrt((2.0 * degree_real + 1.0) * (2.0 * degree_real - 1.0) / divisor)
        fall_factor = jnp.sqrt(jnp.maximum((2.0 * degree_real + 1.0) * ((lower_gap - 1) * (upper_sum - 1)).astype(jnp.float32), 0.0) / (jnp.maximum(2.0 * degree_real - 3.0, 1.0) * divisor))
        current = rise_factor * cosines[None, :] * latest - fall_factor * before
        current = jnp.where(lower_gap == 0, diagonal_start, current)
        current = jnp.where(lower_gap < 0, 0.0, current)
        log_scale = jnp.where(lower_gap == 0, start_scale, log_scale)
        value = current * jnp.exp(log_scale)
        too_big = jnp.abs(current) > 2.0 ** 24
        next_latest = jnp.where(too_big, current * shrink, current)
        next_before = jnp.where(too_big, latest * shrink, latest)
        next_scale = jnp.where(too_big, log_scale + shrink_log, log_scale)
        return ((next_latest, next_before, next_scale), value)
    blank = jnp.zeros_like(diagonal_start)
    _, stacked_rows = lax.scan(recurrence, (blank, blank, blank), jnp.arange(degrees, dtype=jnp.int32), unroll=32)
    return jnp.transpose(stacked_rows, (1, 0, 2))

def reference(fields, conv_weight, spectral_gain, support):
    widened = fields.astype(jnp.float32)
    colatitude = (jnp.arange(NLAT, dtype=jnp.float32) + 0.5) * (math.pi / NLAT)
    cosines = jnp.cos(colatitude)
    cycle_sines = jnp.sin(colatitude)
    cycle_weight = cycle_sines * (math.pi / NLAT)
    transformed = jnp.fft.rfft(widened, axis=1)[:, :M, :]
    spectral_in = jnp.stack([transformed.real / NLON, -transformed.imag / NLON], axis=2).astype(jnp.bfloat16)
    order_block = 32

    def one_block(first_order):
        orders = first_order + jnp.arange(order_block, dtype=jnp.int32)
        legendre = legendre_table(orders, cosines, cycle_sines, M)
        scaled = lax.dynamic_slice_in_dim(spectral_in, first_order, order_block, 1).astype(jnp.float32) * cycle_weight[:, None, None, None]
        forward = jnp.einsum('xmpc,mlx->mplc', scaled, legendre, precision=lax.Precision.HIGHEST)
        filtered = (forward * spectral_gain[None, None, :, :]).astype(jnp.bfloat16)
        returned = jnp.einsum('mplc,mlx->xmpc', filtered.astype(jnp.float32), legendre, precision=lax.Precision.HIGHEST)
        return returned.astype(jnp.bfloat16)
    blocks = lax.map(one_block, jnp.arange(M // order_block, dtype=jnp.int32) * order_block)
    synthesis = jnp.transpose(blocks, (1, 0, 2, 3, 4)).reshape(NLAT, M, 2, C).astype(jnp.float32)
    spectrum = (synthesis[:, :, 0, :] - 1j * synthesis[:, :, 1, :]) * NLON
    spectrum = jnp.pad(spectrum, ((0, 0), (0, NLON // 2 + 1 - M), (0, 0)))
    spectral = jnp.fft.irfft(spectrum, n=NLON, axis=1).astype(jnp.bfloat16)
    padded = jnp.pad(fields, ((1, 1), (0, 0), (0, 0))).astype(jnp.float32)
    spectra = jnp.fft.rfft(padded, axis=1)
    lon_index = jnp.arange(NLON, dtype=jnp.int32)
    offsets = jnp.where(lon_index <= NLON // 2, lon_index, lon_index - NLON)
    kernels = band_weights(offsets[None, :], support[:, None]).astype(jnp.float32)
    kernel_spec = jnp.conj(jnp.fft.rfft(kernels, axis=-1))
    weight_wide = conv_weight.astype(jnp.float32)
    cycle_count = NLAT // N_LAT

    def cycle_block(first_cycle):
        kernel_part = lax.dynamic_slice_in_dim(kernel_spec, first_cycle, cycle_count, 1)
        pooled_rows = []
        for lat_step in range(3):
            source = lax.dynamic_slice_in_dim(spectra, first_cycle + lat_step, cycle_count, 0)
            pooled = jnp.fft.irfft(source[None] * kernel_part[:, :, :, None], n=NLON, axis=2)
            pooled_rows.append(pooled.astype(jnp.bfloat16))
        stacked = jnp.stack(pooled_rows, 0).astype(jnp.float32)
        convolved = jnp.einsum('akyjc,akcd->yjd', stacked, weight_wide)
        spectral_part = lax.dynamic_slice_in_dim(spectral, first_cycle, cycle_count, 0).astype(jnp.float32)
        residual = lax.dynamic_slice_in_dim(widened, first_cycle, cycle_count, 0)
        return (residual + jax.nn.gelu(convolved + spectral_part, approximate=False)).astype(jnp.bfloat16)
    result = lax.map(cycle_block, jnp.arange(NLAT // cycle_count, dtype=jnp.int32) * cycle_count)
    return result.reshape(NLAT, NLON, C)
```

```python
import functools
import math

import jax
import jax.numpy as jnp
import numpy as np
from jax import lax
from jax.experimental import pallas as pl
from jax.experimental.pallas import tpu as pltpu
from jax.sharding import PartitionSpec as P

NLAT = 368
NLON = 1024
M = 512
SMAX = 24
LAT = 16
LON = 32
ROWS = 23
PAD = 24
COLS = 32
HALF = 128
X = LAT * PAD
MESH = pl.DeviceIdType.MESH


def split_pair(table):
    upper_part = table.astype(jnp.bfloat16)
    lower_part = (table - upper_part.astype(jnp.float32)).astype(jnp.bfloat16)
    return upper_part, lower_part


def doubled(table):
    upper = table.astype(jnp.bfloat16)
    lower = (table - upper.astype(np.float32)).astype(jnp.bfloat16)
    return np.concatenate([upper, lower], axis=-1)


def orders_of(bin_index, lat_index):
    first = bin_index + 32 * lat_index
    second = (496 if bin_index == 0 else 512) - first
    return first, second


@functools.lru_cache
def longitude_tables():
    turn = 2.0 * np.pi / NLON
    b = np.arange(32)
    step_one = np.zeros((2, 16, 32))
    for q in range(16):
        step_one[0, q] = np.cos(2 * np.pi * b * q / 32)
        step_one[1, q] = np.sin(2 * np.pi * b * q / 32) if q else (-1.0) ** b
    step_one = step_one.reshape(32, 32)
    r = np.arange(32)
    step_two = np.zeros((16, 2, 2, 16, 2, 32))
    weight = np.zeros((16, 2, 2, 16))
    for q in range(16):
        for a in range(16):
            for u, m in enumerate(orders_of(q, a)):
                cos, sin = np.cos(turn * ((m * r) % NLON)), np.sin(turn * ((m * r) % NLON))
                weight[q, u, :, a] = 1.0 if m == 0 else 2.0
                if q == 0:
                    step_two[q, u, 0, a, u] = cos
                    step_two[q, u, 1, a, u] = sin
                else:
                    sign = 1.0 if u == 0 else -1.0
                    step_two[q, u, 0, a, 0] = cos
                    step_two[q, u, 0, a, 1] = -sign * sin
                    step_two[q, u, 1, a, 0] = sin
                    step_two[q, u, 1, a, 1] = sign * cos
    step_two = step_two.reshape(16, 64, 64)
    back = np.swapaxes(step_two * weight.reshape(16, 64, 1), 1, 2)
    f32 = np.float32
    return (
        doubled(step_one.astype(f32)),
        doubled((step_two / NLON).astype(f32)),
        doubled(back.astype(f32)),
        doubled(step_one.T.astype(f32)),
    )


@functools.lru_cache
def cycle_tables():
    t = np.pi * (np.arange(NLAT) + 0.5) / NLAT
    cos = np.zeros((LAT, PAD))
    log_sin = np.full((LAT, PAD), 0.0)
    weight = np.zeros((LAT, PAD))
    cos[:, :ROWS] = np.cos(t).reshape(LAT, ROWS)
    log_sin[:, :ROWS] = np.log(np.sin(t)).reshape(LAT, ROWS)
    weight[:, :ROWS] = (np.sin(t) * np.pi / NLAT).reshape(LAT, ROWS)
    valid = np.zeros((LAT, PAD))
    valid[:, :ROWS] = 1.0
    k = np.arange(1, M)
    log_norm = np.concatenate([[0.0], np.cumsum(np.log((2 * k - 1) / (2 * k)))])
    log_norm = 0.5 * np.log((2 * np.arange(M) + 1) / 2) + 0.5 * log_norm
    f32 = np.float32
    return (
        cos.reshape(1, X).astype(f32),
        log_sin.reshape(1, X).astype(f32),
        weight.astype(f32),
        valid.reshape(1, X).astype(f32),
        log_norm.astype(f32),
    )


def legendre_kernel(orders, rise, fall, cos_ref, start_ref, scale_ref, upper, lower, table):
    first = lax.broadcasted_iota(jnp.int32, (2, X), 0) == 0
    cosines = cos_ref[...]
    diagonal = start_ref[...]
    start_scale = scale_ref[...]
    order = [orders[0], orders[1]]

    def pair(one, two):
        return jnp.where(first, one, two)

    def steps(block, state):
        latest, before, log_scale = state
        factor = jnp.exp(log_scale)
        for k in range(4):
            degree = block * 4 + k
            up = pair(rise[0, degree], rise[1, degree]) * cosines
            down = pair(fall[0, degree], fall[1, degree])
            on = pair(
                jnp.where(order[0] == degree, 1.0, 0.0), jnp.where(order[1] == degree, 1.0, 0.0)
            )
            current = up * latest + (on * diagonal - down * before)
            value = current * factor
            for lane in range(X // HALF):
                table[lane, pl.ds(2 * degree, 2), :] = value[:, lane * HALF : (lane + 1) * HALF]
            latest, before = current, latest
        too_big = jnp.abs(latest) > 2.0**24
        shrink = jnp.where(too_big, 2.0**-24, 1.0)
        log_scale = jnp.where(too_big, log_scale + 24.0 * math.log(2.0), log_scale)
        return latest * shrink, before * shrink, log_scale

    blank = jnp.zeros((2, X), jnp.float32)
    lax.fori_loop(0, M // 4, steps, (blank, blank, start_scale))
    for u in range(2):
        for lane in range(X // HALF):
            rows = table[lane, pl.ds(u, M, stride=2), :]
            high, low = split_pair(rows)
            upper[u, :, lane * HALF : (lane + 1) * HALF] = high
            lower[u, :, lane * HALF : (lane + 1) * HALF] = low


def legendre_pair(bin_index, lat_index):
    cos, log_sin, _, valid, log_norm = cycle_tables()
    first = bin_index + 32 * lat_index
    orders = jnp.stack([first, jnp.where(bin_index == 0, 496, 512) - first]).astype(jnp.int32)
    log_start = jnp.asarray(log_norm)[orders][:, None] + orders.astype(jnp.float32)[:, None] * log_sin
    start_scale = jnp.minimum(log_start, 0.0)
    diagonal = jnp.exp(log_start - start_scale) * valid
    degree = jnp.arange(M, dtype=jnp.int32)[None, :]
    degree_real = degree.astype(jnp.float32)
    lower_gap = degree - orders[:, None]
    upper_sum = degree + orders[:, None]
    inside = lower_gap > 0
    divisor = jnp.where(inside, lower_gap * upper_sum, 1).astype(jnp.float32)
    rise = jnp.sqrt((2.0 * degree_real + 1.0) * (2.0 * degree_real - 1.0) / divisor)
    fall = jnp.sqrt(
        (2.0 * degree_real + 1.0)
        * ((lower_gap - 1) * (upper_sum - 1)).astype(jnp.float32)
        / (jnp.maximum(2.0 * degree_real - 3.0, 1.0) * divisor)
    )
    rise = jnp.where(inside, rise, 0.0)
    fall = jnp.where(inside, fall, 0.0)
    smem = pl.BlockSpec(memory_space=pltpu.SMEM)
    vmem = pl.BlockSpec(memory_space=pltpu.VMEM)
    return pl.pallas_call(
        legendre_kernel,
        out_shape=[jax.ShapeDtypeStruct((2, M, X), jnp.bfloat16)] * 2,
        in_specs=[smem, smem, smem, vmem, vmem, vmem],
        out_specs=[vmem, vmem],
        scratch_shapes=[pltpu.VMEM((X // HALF, 2 * M, HALF), jnp.float32)],
        compiler_params=pltpu.CompilerParams(vmem_limit_bytes=48 * 2**20),
        cost_estimate=pl.CostEstimate(flops=10_000_000, bytes_accessed=1_600_000, transcendentals=0),
    )(orders, rise, fall, jnp.asarray(cos), diagonal, start_scale)


def dot(left, right):
    return jnp.dot(left, right, preferred_element_type=jnp.float32)


def twice(block):
    return jnp.concatenate([block, block], axis=0)


def block_kernel(
    fields, conv_weight, gain, support, upper, lower, one, two, three, four, weight,
    out,
    s1, g1, s2, g2, s3, g3, s4, g4, s5, g5, s6, g6, wide, pooled, convolved, near, far, send, recv,
):
    lat = lax.axis_index("lat")
    lon = lax.axis_index("lon")
    f32, bf16 = jnp.float32, jnp.bfloat16

    barrier = pltpu.get_barrier_semaphore()

    def greet_lon(step, _):
        pl.semaphore_signal(
            barrier, inc=1, device_id=(lat, (lon + step) % LON), device_id_type=MESH
        )
        return 0

    def greet_lat(step, _):
        pl.semaphore_signal(
            barrier, inc=1, device_id=((lat + step) % LAT, lon), device_id_type=MESH
        )
        return 0

    lax.fori_loop(1, LON, greet_lon, 0)
    lax.fori_loop(1, LAT, greet_lat, 0)
    pl.semaphore_wait(barrier, LON + LAT - 2)

    def send_lon(source, target, index):
        def one_peer(step, _):
            peer = (lon + step) % LON
            pltpu.make_async_remote_copy(
                src_ref=source.at[peer], dst_ref=target.at[lon], send_sem=send.at[index],
                recv_sem=recv.at[index], device_id=(lat, peer), device_id_type=MESH,
            ).start()
            return 0

        lax.fori_loop(1, LON, one_peer, 0)
        target[lon] = source[lon]

    def send_lat(source, target, index):
        def one_peer(step, _):
            peer = (lat + step) % LAT
            pltpu.make_async_remote_copy(
                src_ref=source.at[peer], dst_ref=target.at[lat], send_sem=send.at[index],
                recv_sem=recv.at[index], device_id=(peer, lon), device_id_type=MESH,
            ).start()
            return 0

        lax.fori_loop(1, LAT, one_peer, 0)
        target[lat] = source[lat]

    def whole(source, target, index, count):
        return pltpu.make_async_remote_copy(
            src_ref=source.at[pl.ds(0, count)], dst_ref=target.at[pl.ds(0, count)],
            send_sem=send.at[index], recv_sem=recv.at[index],
            device_id=((lat + 1) % LAT, (lon + 1) % LON), device_id_type=MESH,
        )

    for half in range(2):
        lanes = slice(half * HALF, (half + 1) * HALF)
        near[half, pl.ds(0, ROWS * COLS), :] = fields[:, :, lanes].astype(f32).reshape(ROWS * COLS, HALF)
        near[half, pl.ds(ROWS * COLS, COLS), :] = jnp.zeros((COLS, HALF), f32)

    def pack_residue(r, _):
        rows = [near[half, pl.ds(r, PAD, stride=COLS), :] for half in range(2)]
        s1[r] = jnp.concatenate(rows, axis=0).astype(bf16)
        return 0

    lax.fori_loop(0, LON, pack_residue, 0)
    send_lon(s1, g1, 0)

    halo_right = pltpu.make_async_remote_copy(
        src_ref=fields, dst_ref=wide.at[pl.ds(1, ROWS), pl.ds(0, COLS), :], send_sem=send.at[6],
        recv_sem=recv.at[6], device_id=(lat, (lon + 1) % LON), device_id_type=MESH,
    )
    halo_left = pltpu.make_async_remote_copy(
        src_ref=fields, dst_ref=wide.at[pl.ds(1, ROWS), pl.ds(2 * COLS, COLS), :],
        send_sem=send.at[7], recv_sem=recv.at[7], device_id=(lat, (lon + LON - 1) % LON),
        device_id_type=MESH,
    )
    halo_right.start()
    halo_left.start()
    wide[1 : ROWS + 1, COLS : 2 * COLS, :] = fields[...]

    whole(s1, g1, 0, LON - 1).wait_recv()
    far[...] = g1[...].astype(f32).reshape(LON * 2 * PAD, HALF)
    table = one[...]
    for group in range(6):
        block = jnp.concatenate(
            [far[pl.ds(group * 8 + n, 32, stride=48), :] for n in range(8)], axis=1
        ).astype(bf16)
        result = dot(table, twice(block))
        for n in range(8):
            half, row = divmod(group * 8 + n, PAD)
            lanes = slice(n * HALF, (n + 1) * HALF)
            for part in range(2):
                near[0, pl.ds(half * 48 + part * PAD + row, 16, stride=96), :] = result[
                    part * 16 : part * 16 + 16, lanes
                ]
    s2[...] = near[0].reshape(LON, 48, HALF).astype(bf16)
    send_lon(s2, g2, 1)

    halo_right.wait_recv()
    halo_left.wait_recv()
    halo_down = pltpu.make_async_remote_copy(
        src_ref=wide.at[ROWS], dst_ref=wide.at[0], send_sem=send.at[8], recv_sem=recv.at[8],
        device_id=((lat + 1) % LAT, lon), device_id_type=MESH,
    )
    halo_up = pltpu.make_async_remote_copy(
        src_ref=wide.at[1], dst_ref=wide.at[ROWS + 1], send_sem=send.at[9], recv_sem=recv.at[9],
        device_id=((lat + LAT - 1) % LAT, lon), device_id_type=MESH,
    )
    halo_down.start()
    halo_up.start()

    whole(s2, g2, 1, LON - 1).wait_recv()
    far[...] = g2[...].astype(f32).reshape(LON * 48, HALF)
    table = two[...]
    for group in range(3):
        block = jnp.concatenate(
            [
                jnp.concatenate(
                    [far[pl.ds(part * PAD + group * 8 + n, 32, stride=48), :] for part in range(2)],
                    axis=0,
                )
                for n in range(8)
            ],
            axis=1,
        ).astype(bf16)
        result = dot(table, twice(block))
        for n in range(8):
            row = group * 8 + n
            scaled = result[:, n * HALF : (n + 1) * HALF] * weight[pl.ds(row, 1), :]
            for k in range(4):
                near[0, pl.ds(k * PAD + row, 16, stride=96), :] = scaled[k * 16 : k * 16 + 16]
    s3[...] = near[0].reshape(LAT, 96, HALF).astype(bf16)
    send_lat(s3, g3, 2)

    halo_down.wait_recv()
    halo_up.wait_recv()
    halo_right.wait_send()
    halo_left.wait_send()
    halo_down.wait_send()
    halo_up.wait_send()
    edge = jnp.full((3 * COLS, 2 * HALF), lat, jnp.int32)
    wide[0] = jnp.where(edge > 0, wide[0].astype(f32), 0.0).astype(bf16)
    wide[ROWS + 1] = jnp.where(edge < LAT - 1, wide[ROWS + 1].astype(f32), 0.0).astype(bf16)
    source = lax.broadcasted_iota(jnp.int32, (COLS, 3 * COLS), 1)
    target = lax.broadcasted_iota(jnp.int32, (COLS, 3 * COLS), 0)
    offset = source - target - COLS
    offset_real = offset.astype(f32)
    distance = jnp.abs(offset)
    distance_real = distance.astype(f32)

    def pool(y, _):
        half_width = jnp.full((COLS, 3 * COLS), support[y], jnp.int32)
        span_len = (half_width + 1).astype(f32)
        inside = distance <= half_width
        triangle = jnp.where(inside, (span_len - distance_real) / span_len, 0.0)
        odd_basis = offset_real * triangle / span_len
        box_basis = jnp.where(inside, 1.0, 0.0) / jnp.sqrt(2.0 * half_width.astype(f32) + 1.0)
        band = jnp.concatenate([triangle, odd_basis, box_basis], axis=0).astype(bf16)
        start = pl.multiple_of(y * COLS, COLS)
        for a in range(3):
            basis = dot(band, wide[y + a]).astype(bf16)
            for k in range(3):
                pooled[pl.ds(start, COLS), pl.ds((a * 3 + k) * 256, 256)] = basis[
                    k * COLS : (k + 1) * COLS
                ]
        return 0

    lax.fori_loop(0, ROWS, pool, 0)

    whole(s3, g3, 2, LAT - 1).wait_recv()
    gains = jnp.concatenate([gain[...], gain[...]], axis=1)
    for u in range(2):
        data = jnp.concatenate(
            [
                g3[:, (2 * u + p) * PAD : (2 * u + p + 1) * PAD, :].astype(f32).reshape(X, HALF)
                for p in range(2)
            ],
            axis=1,
        ).astype(bf16)
        high, low = upper[u], lower[u]
        analysis = dot(high, data) + dot(low, data)
        filtered = (analysis * gains).astype(bf16)
        back = (((0,), (0,)), ((), ()))
        synthesis = lax.dot_general(
            high, filtered, back, preferred_element_type=f32
        ) + lax.dot_general(low, filtered, back, preferred_element_type=f32)
        for p in range(2):
            lanes = synthesis[:, p * HALF : (p + 1) * HALF].reshape(LAT, PAD, HALF)
            for a in range(LAT):
                near[1, pl.ds(a * 96 + (2 * u + p) * PAD, PAD), :] = lanes[a]
    s4[...] = near[1].reshape(LAT, 96, HALF).astype(bf16)
    send_lat(s4, g4, 3)

    rows = ROWS * COLS // 4
    for part in range(4):
        convolved[part * rows : (part + 1) * rows, :] = dot(
            pooled[part * rows : (part + 1) * rows, :], conv_weight[...]
        )

    whole(s4, g4, 3, LAT - 1).wait_recv()
    far[...] = g4[...].astype(f32).reshape(LAT * 96, HALF)
    table = three[...]
    for group in range(3):
        block = jnp.concatenate(
            [
                jnp.concatenate(
                    [far[pl.ds(k * PAD + group * 8 + n, 16, stride=96), :] for k in range(4)], axis=0
                )
                for n in range(8)
            ],
            axis=1,
        ).astype(bf16)
        result = dot(table, twice(block))
        for n in range(8):
            row = group * 8 + n
            for part in range(2):
                near[0, pl.ds(part * PAD + row, 32, stride=48), :] = result[
                    part * 32 : part * 32 + 32, n * HALF : (n + 1) * HALF
                ]
    s5[...] = near[0].reshape(LON, 48, HALF).astype(bf16)
    send_lon(s5, g5, 4)

    whole(s5, g5, 4, LON - 1).wait_recv()
    far[...] = g5[...].astype(f32).reshape(LON * 48, HALF)
    table = four[...]
    for group in range(6):
        block = jnp.concatenate(
            [
                jnp.concatenate(
                    [
                        far[
                            pl.ds(
                                (group * 8 + n) // PAD * 48 + part * PAD + (group * 8 + n) % PAD,
                                16, stride=96,
                            ),
                            :,
                        ]
                        for part in range(2)
                    ],
                    axis=0,
                )
                for n in range(8)
            ],
            axis=1,
        ).astype(bf16)
        result = dot(table, twice(block))
        for n in range(8):
            near[0, pl.ds(group * 8 + n, 32, stride=48), :] = result[
                :, n * HALF : (n + 1) * HALF
            ]
    s6[...] = near[0].reshape(LON, 48, HALF).astype(bf16)
    send_lon(s6, g6, 5)

    whole(s6, g6, 5, LON - 1).wait_recv()
    far[...] = g6[...].astype(f32).reshape(LON * 48, HALF)

    def finish(y, _):
        spectral = jnp.concatenate(
            [far[pl.ds(half * PAD + y, 32, stride=48), :] for half in range(2)], axis=1
        )
        start = pl.multiple_of(y * COLS, COLS)
        total = convolved[pl.ds(start, COLS), :] + spectral
        gelu = 0.5 * total * (1.0 + lax.erf(total * math.sqrt(0.5)))
        out[y] = (fields[y].astype(f32) + gelu).astype(bf16)
        return 0

    lax.fori_loop(0, ROWS, finish, 0)

    whole(s1, g1, 0, LON - 1).wait_send()
    whole(s2, g2, 1, LON - 1).wait_send()
    whole(s3, g3, 2, LAT - 1).wait_send()
    whole(s4, g4, 3, LAT - 1).wait_send()
    whole(s5, g5, 4, LON - 1).wait_send()
    whole(s6, g6, 5, LON - 1).wait_send()


def per_device(fields, conv_weight, spectral_gain, support):
    lat = lax.axis_index("lat")
    lon = lax.axis_index("lon")
    bin_index, half = lon // 2, lon % 2
    upper, lower = legendre_pair(bin_index, lat)
    one, two, three, four = longitude_tables()
    two = lax.dynamic_index_in_dim(jnp.asarray(two), bin_index, 0, keepdims=False)
    three = lax.dynamic_index_in_dim(jnp.asarray(three), bin_index, 0, keepdims=False)
    weight = lax.dynamic_index_in_dim(jnp.asarray(cycle_tables()[2]), lat, 0, keepdims=False)
    weight = jnp.broadcast_to(weight[:, None], (PAD, HALF))
    gain = lax.dynamic_slice_in_dim(spectral_gain, half * HALF, HALF, 1)
    vmem = pl.BlockSpec(memory_space=pltpu.VMEM)
    smem = pl.BlockSpec(memory_space=pltpu.SMEM)
    by_lon = pltpu.VMEM((LON, 48, HALF), jnp.bfloat16)
    by_lat = pltpu.VMEM((LAT, 96, HALF), jnp.bfloat16)
    return pl.pallas_call(
        block_kernel,
        out_shape=jax.ShapeDtypeStruct(fields.shape, fields.dtype),
        in_specs=[vmem, vmem, vmem, smem] + [vmem] * 7,
        out_specs=vmem,
        scratch_shapes=[by_lon] * 4
        + [by_lat] * 4
        + [by_lon] * 4
        + [
            pltpu.VMEM((ROWS + 2, 3 * COLS, 256), jnp.bfloat16),
            pltpu.VMEM((ROWS * COLS, 9 * 256), jnp.bfloat16),
            pltpu.VMEM((ROWS * COLS, 256), jnp.float32),
            pltpu.VMEM((2, LON * 48, HALF), jnp.float32),
            pltpu.VMEM((LON * 48, HALF), jnp.float32),
            pltpu.SemaphoreType.DMA((10,)),
            pltpu.SemaphoreType.DMA((10,)),
        ],
        compiler_params=pltpu.CompilerParams(
            collective_id=0, has_side_effects=True, vmem_limit_bytes=48 * 2**20
        ),
    )(
        fields, conv_weight.reshape(9 * 256, 256), gain, support, upper, lower,
        jnp.asarray(one), two, three, jnp.asarray(four), weight,
    )


def solution(mesh):
    placed = (P("lat", "lon", None), P(), P(), P("lat"))
    return jax.shard_map(
        per_device, mesh=mesh, in_specs=placed, out_specs=P("lat", "lon", None), check_vma=False
    )
```

```python
import functools
import math

import jax
import jax.numpy as jnp
import numpy as np
from jax import lax
from jax.experimental import pallas as pl
from jax.experimental.pallas import tpu as pltpu
from jax.sharding import PartitionSpec as P

NLAT = 368
NLON = 1024
M = 512
SMAX = 24
LAT = 16
LON = 32
ROWS = 23
PAD = 24
COLS = 32
HALF = 128
X = LAT * PAD
MESH = pl.DeviceIdType.MESH


def split_pair(table):
    upper_part = table.astype(jnp.bfloat16)
    lower_part = (table - upper_part.astype(jnp.float32)).astype(jnp.bfloat16)
    return upper_part, lower_part


def doubled(table):
    upper = table.astype(jnp.bfloat16)
    lower = (table - upper.astype(np.float32)).astype(jnp.bfloat16)
    return np.concatenate([upper, lower], axis=-1)


def orders_of(bin_index, lat_index):
    first = bin_index + 32 * lat_index
    second = (496 if bin_index == 0 else 512) - first
    return first, second


@functools.lru_cache
def longitude_tables():
    turn = 2.0 * np.pi / NLON
    b = np.arange(32)
    step_one = np.zeros((2, 16, 32))
    for q in range(16):
        step_one[0, q] = np.cos(2 * np.pi * b * q / 32)
        step_one[1, q] = np.sin(2 * np.pi * b * q / 32) if q else (-1.0) ** b
    step_one = step_one.reshape(32, 32)
    r = np.arange(32)
    step_two = np.zeros((16, 2, 2, 16, 2, 32))
    weight = np.zeros((16, 2, 2, 16))
    for q in range(16):
        for a in range(16):
            for u, m in enumerate(orders_of(q, a)):
                cos, sin = np.cos(turn * ((m * r) % NLON)), np.sin(turn * ((m * r) % NLON))
                weight[q, u, :, a] = 1.0 if m == 0 else 2.0
                if q == 0:
                    step_two[q, u, 0, a, u] = cos
                    step_two[q, u, 1, a, u] = sin
                else:
                    sign = 1.0 if u == 0 else -1.0
                    step_two[q, u, 0, a, 0] = cos
                    step_two[q, u, 0, a, 1] = -sign * sin
                    step_two[q, u, 1, a, 0] = sin
                    step_two[q, u, 1, a, 1] = sign * cos
    step_two = step_two.reshape(16, 2, 2, 8, 2, 64).transpose(0, 2, 4, 1, 3, 5).reshape(16, 64, 64)
    weight = weight.reshape(16, 2, 2, 8, 2).transpose(0, 2, 4, 1, 3).reshape(16, 64, 1)
    back = np.swapaxes(step_two * weight, 1, 2)
    f32 = np.float32
    return (
        doubled(step_one.astype(f32)),
        doubled((step_two / NLON).astype(f32)),
        doubled(back.astype(f32)),
        doubled(step_one.T.astype(f32)),
    )


@functools.lru_cache
def cycle_tables():
    t = np.pi * (np.arange(NLAT) + 0.5) / NLAT
    f32 = np.float32

    def placed(values):
        padded = np.zeros((LAT, PAD))
        padded[:, :ROWS] = values.reshape(LAT, ROWS)
        return padded.reshape(4, 2, 2, PAD).transpose(0, 2, 1, 3).astype(f32)

    weight = placed(np.sin(t) * np.pi / NLAT).reshape(8, 2, PAD).transpose(0, 2, 1)
    weight = np.repeat(weight, 64, axis=2)
    k = np.arange(1, M)
    log_norm = np.concatenate([[0.0], np.cumsum(np.log((2 * k - 1) / (2 * k)))])
    log_norm = 0.5 * np.log((2 * np.arange(M) + 1) / 2) + 0.5 * log_norm
    rows = np.stack(
        [placed(np.cos(t)).reshape(X), placed(np.log(np.sin(t))).reshape(X), placed(np.ones(NLAT)).reshape(X)]
    )
    return rows, weight, log_norm.reshape(1, M).astype(f32)


def dot(left, right):
    return jnp.dot(left, right, preferred_element_type=jnp.float32)


def twice(block):
    return jnp.concatenate([block, block], axis=0)


def trade(first, second):
    low = lax.broadcasted_iota(jnp.int32, first.shape, 1) < 64
    return (
        jnp.where(low, first, pltpu.roll(second, 64, axis=1)),
        jnp.where(low, pltpu.roll(first, 64, axis=1), second),
    )


def legendre_orders(bin_index, owner, cycle_rows, log_norm, up_table, down_table, table, legendre):
    f32 = jnp.float32

    def order_rows(slot):
        first = bin_index + 64 * owner + 32 * (slot // 2)
        return jnp.where(slot % 2 == 0, first, jnp.where(bin_index == 0, 496, 512) - first)

    def coefficients(block, _):
        row = lax.broadcasted_iota(jnp.int32, (128, HALF), 0)
        degree = (block * 32 + row // 4).astype(f32)
        order = order_rows(row % 4).astype(f32)
        gap, total = degree - order, degree + order
        inside = gap > 0.5
        odd = 2.0 * degree + 1.0
        shared = odd / jnp.where(inside, gap * total, 1.0)
        rise = jnp.sqrt(shared * jnp.maximum(2.0 * degree - 1.0, 0.0))
        fall = jnp.sqrt(
            shared * jnp.maximum((gap - 1.0) * (total - 1.0), 0.0) / jnp.maximum(2.0 * degree - 3.0, 1.0)
        )
        start = pl.multiple_of(block * 128, 128)
        up_table[pl.ds(start, 128), :] = jnp.where(inside, rise, 0.0)
        down_table[pl.ds(start, 128), :] = jnp.where(inside, fall, 0.0)
        return 0

    lax.fori_loop(0, 16, coefficients, 0)
    order = order_rows(lax.broadcasted_iota(jnp.int32, (4, X), 0))
    wide_order = order_rows(lax.broadcasted_iota(jnp.int32, (4, M), 0))
    column = lax.broadcasted_iota(jnp.int32, (4, M), 1)
    norm = jnp.sum(jnp.where(column == wide_order, log_norm[...], 0.0), axis=1, keepdims=True)
    cosines = jnp.broadcast_to(cycle_rows[pl.ds(0, 1), :], (4, X))
    log_start = norm + order.astype(f32) * cycle_rows[pl.ds(1, 1), :]
    start_scale = jnp.minimum(log_start, 0.0)
    diagonal = jnp.exp(log_start - start_scale) * cycle_rows[pl.ds(2, 1), :]

    def spread(rows):
        return jnp.concatenate([rows] * (X // HALF), axis=1)

    def steps(block, state):
        latest, before, log_scale = state
        factor = jnp.exp(log_scale)
        for k in range(4):
            degree = block * 4 + k
            up = spread(up_table[pl.ds(4 * degree, 4), :]) * cosines
            down = spread(down_table[pl.ds(4 * degree, 4), :])
            current = up * latest + (jnp.where(order == degree, diagonal, 0.0) - down * before)
            value = current * factor
            for lane in range(X // HALF):
                table[lane, pl.ds(4 * degree, 4), :] = value[:, lane * HALF : (lane + 1) * HALF]
            latest, before = current, latest
        too_big = jnp.abs(latest) > 2.0**24
        shrink = jnp.where(too_big, 2.0**-24, 1.0)
        log_scale = jnp.where(too_big, log_scale + 24.0 * math.log(2.0), log_scale)
        return latest * shrink, before * shrink, log_scale

    blank = jnp.zeros((4, X), f32)
    lax.fori_loop(0, M // 4, steps, (blank, blank, start_scale))
    for slot in range(4):
        for lane in range(X // HALF):
            legendre[slot, :, lane * HALF : (lane + 1) * HALF] = table[
                lane, pl.ds(slot, M, stride=4), :
            ].astype(jnp.bfloat16)


def block_kernel(
    fields, conv_weight, gain, support, one, two, three, four, cycle_rows, weight, log_norm,
    out,
    s1, g1, s2, g2, s3, g3, s4, g4, s5, g5, s6, g6, wide, pooled, convolved, near, far,
    up_table, down_table, table, legendre, gains, send, recv,
):
    lat = lax.axis_index("lat")
    lon = lax.axis_index("lon")
    hemi = lat // 2 % 2
    owner = lat // 4 * 2 + lat % 2
    spot = hemi * LON + lon
    bin_index, half_index = lon // 2, lon % 2
    f32, bf16 = jnp.float32, jnp.bfloat16

    def double_peer(step):
        index = (spot + step) % (2 * LON)
        return index, (lat // 4 * 4 + index // LON * 2 + lat % 2, index % LON)

    def owner_peer(step):
        index = (owner + step) % 8
        return index, (index // 2 * 4 + hemi * 2 + index % 2, lon)

    def ring_peer(step):
        index = (lon + step) % LON
        return index, (lat, index)

    barrier = pltpu.get_barrier_semaphore()

    def greet(peer_of):
        def one_peer(step, _):
            pl.semaphore_signal(barrier, inc=1, device_id=peer_of(step)[1], device_id_type=MESH)
            return 0

        return one_peer

    lax.fori_loop(1, 2 * LON, greet(double_peer), 0)
    lax.fori_loop(1, 8, greet(owner_peer), 0)
    for step in (1, LAT - 1):
        pl.semaphore_signal(
            barrier, inc=1, device_id=((lat + step) % LAT, lon), device_id_type=MESH
        )

    def exchange(source, target, index, peer_of, mine, count):
        def one_peer(step, _):
            peer, device = peer_of(step)
            pltpu.make_async_remote_copy(
                src_ref=source.at[peer], dst_ref=target.at[mine], send_sem=send.at[index],
                recv_sem=recv.at[index], device_id=device, device_id_type=MESH,
            ).start()
            return 0

        lax.fori_loop(1, count, one_peer, 0)
        target[mine] = source[mine]

    def whole(source, target, index, count):
        return pltpu.make_async_remote_copy(
            src_ref=source.at[pl.ds(0, count)], dst_ref=target.at[pl.ds(0, count)],
            send_sem=send.at[index], recv_sem=recv.at[index],
            device_id=(lat, (lon + 1) % LON), device_id_type=MESH,
        )

    for half in range(2):
        lanes = slice(half * HALF, (half + 1) * HALF)
        near[half, pl.ds(0, ROWS * COLS), :] = fields[:, :, lanes].astype(f32).reshape(ROWS * COLS, HALF)
        near[half, pl.ds(ROWS * COLS, COLS), :] = jnp.zeros((COLS, HALF), f32)

    def pack_residue(r, _):
        rows = [near[half, pl.ds(r, PAD, stride=COLS), :] for half in range(2)]
        s1[r] = jnp.concatenate(rows, axis=0).astype(bf16)
        return 0

    lax.fori_loop(0, LON, pack_residue, 0)
    pl.semaphore_wait(barrier, 2 * LON - 1 + 7 + 2)
    exchange(s1, g1, 0, ring_peer, lon, LON)

    legendre_orders(
        bin_index, owner, cycle_rows, log_norm, up_table, down_table, table, legendre
    )
    own_gain = gain[:, pl.ds(pl.multiple_of(half_index * HALF, HALF), HALF)]
    turned = pltpu.roll(own_gain, 64, axis=1)
    lower_lanes = lax.broadcasted_iota(jnp.int32, (M, HALF), 1) // 64
    gains[...] = jnp.where(lower_lanes == hemi, own_gain, turned)
    wide[1 : ROWS + 1, COLS : 2 * COLS, :] = fields[...]

    whole(s1, g1, 0, LON - 1).wait_recv()
    far[...] = g1[...].astype(f32).reshape(LON * 48, HALF)
    matrix = one[...]
    for group in range(6):
        block = jnp.concatenate(
            [far[pl.ds(group * 8 + n, 32, stride=48), :] for n in range(8)], axis=1
        ).astype(bf16)
        result = dot(matrix, twice(block))
        for n in range(8):
            half, row = divmod(group * 8 + n, PAD)
            lanes = slice(n * HALF, (n + 1) * HALF)
            quarters = trade(result[0:16, lanes], result[16:32, lanes])
            for g in range(2):
                near[0, pl.ds((g * LON + half) * PAD + row, 16, stride=48), :] = quarters[g]
    s2[...] = near[0].reshape(2 * LON, PAD, HALF).astype(bf16)
    exchange(s2, g2, 1, double_peer, spot, 2 * LON)

    halo_right = pltpu.make_async_remote_copy(
        src_ref=fields, dst_ref=wide.at[pl.ds(1, ROWS), pl.ds(0, COLS), :], send_sem=send.at[6],
        recv_sem=recv.at[6], device_id=(lat, (lon + 1) % LON), device_id_type=MESH,
    )
    halo_left = pltpu.make_async_remote_copy(
        src_ref=fields, dst_ref=wide.at[pl.ds(1, ROWS), pl.ds(2 * COLS, COLS), :],
        send_sem=send.at[7], recv_sem=recv.at[7], device_id=(lat, (lon + LON - 1) % LON),
        device_id_type=MESH,
    )

    whole(s2, g2, 1, 2 * LON - 1).wait_recv()
    halo_right.start()
    halo_left.start()
    far[...] = g2[...].astype(f32).reshape(2 * LON * PAD, HALF)
    matrix = two[bin_index]
    weights = weight[owner]
    for group in range(3):
        columns = []
        for n in range(8):
            row = group * 8 + n
            columns.append(
                jnp.concatenate(
                    trade(
                        far[pl.ds(row, 32, stride=PAD), :],
                        far[pl.ds(LON * PAD + row, 32, stride=PAD), :],
                    ),
                    axis=0,
                )
            )
        result = dot(matrix, twice(jnp.concatenate(columns, axis=1).astype(bf16)))
        for n in range(8):
            row = group * 8 + n
            scaled = result[:, n * HALF : (n + 1) * HALF] * weights[row : row + 1, :]
            sides = trade(scaled[0:32], scaled[32:64])
            for g in range(2):
                for slot in range(4):
                    near[0, pl.ds(slot * 48 + g * PAD + row, 8, stride=192), :] = sides[g][
                        slot * 8 : slot * 8 + 8
                    ]
    s3[...] = near[0].reshape(8, 192, HALF).astype(bf16)
    exchange(s3, g3, 2, owner_peer, owner, 8)

    whole(s3, g3, 2, 7).wait_recv()
    for slot in range(4):
        data = g3[:, slot * 48 : slot * 48 + 48, :].reshape(X, HALF)
        filtered = (dot(legendre[slot], data) * gains[...]).astype(bf16)
        synthesis = lax.dot_general(
            legendre[slot], filtered, (((0,), (0,)), ((), ())), preferred_element_type=f32
        )
        s4[:, slot * 48 : slot * 48 + 48, :] = synthesis.reshape(8, 48, HALF).astype(bf16)
    exchange(s4, g4, 3, owner_peer, owner, 8)

    halo_right.wait_recv()
    halo_left.wait_recv()
    halo_down = pltpu.make_async_remote_copy(
        src_ref=wide.at[ROWS], dst_ref=wide.at[0], send_sem=send.at[8], recv_sem=recv.at[8],
        device_id=((lat + 1) % LAT, lon), device_id_type=MESH,
    )
    halo_up = pltpu.make_async_remote_copy(
        src_ref=wide.at[1], dst_ref=wide.at[ROWS + 1], send_sem=send.at[9], recv_sem=recv.at[9],
        device_id=((lat + LAT - 1) % LAT, lon), device_id_type=MESH,
    )
    halo_down.start()
    halo_up.start()

    whole(s4, g4, 3, 7).wait_recv()
    far[...] = g4[...].astype(f32).reshape(8 * 192, HALF)
    matrix = three[bin_index]
    for group in range(3):
        columns = []
        for n in range(8):
            row = group * 8 + n
            sides = [
                jnp.concatenate(
                    [
                        far[pl.ds(slot * 48 + g * PAD + row, 8, stride=192), :]
                        for slot in range(4)
                    ],
                    axis=0,
                )
                for g in range(2)
            ]
            columns.append(jnp.concatenate(trade(*sides), axis=0))
        result = dot(matrix, twice(jnp.concatenate(columns, axis=1).astype(bf16)))
        for n in range(8):
            row = group * 8 + n
            lanes = slice(n * HALF, (n + 1) * HALF)
            sides = trade(result[0:32, lanes], result[32:64, lanes])
            for g in range(2):
                near[0, pl.ds(g * LON * PAD + row, 32, stride=PAD), :] = sides[g]
    s5[...] = near[0].reshape(2 * LON, PAD, HALF).astype(bf16)
    exchange(s5, g5, 4, double_peer, spot, 2 * LON)

    halo_down.wait_recv()
    halo_up.wait_recv()
    halo_right.wait_send()
    halo_left.wait_send()
    halo_down.wait_send()
    halo_up.wait_send()
    edge = jnp.full((3 * COLS, 2 * HALF), lat, jnp.int32)
    wide[0] = jnp.where(edge > 0, wide[0].astype(f32), 0.0).astype(bf16)
    wide[ROWS + 1] = jnp.where(edge < LAT - 1, wide[ROWS + 1].astype(f32), 0.0).astype(bf16)
    source = lax.broadcasted_iota(jnp.int32, (COLS, 3 * COLS), 1)
    target = lax.broadcasted_iota(jnp.int32, (COLS, 3 * COLS), 0)
    offset = source - target - COLS
    offset_real = offset.astype(f32)
    distance = jnp.abs(offset)
    distance_real = distance.astype(f32)

    def pool(y, _):
        half_width = jnp.full((COLS, 3 * COLS), support[y], jnp.int32)
        span_len = (half_width + 1).astype(f32)
        inside = distance <= half_width
        triangle = jnp.where(inside, (span_len - distance_real) / span_len, 0.0)
        odd_basis = offset_real * triangle / span_len
        box_basis = jnp.where(inside, 1.0, 0.0) / jnp.sqrt(2.0 * half_width.astype(f32) + 1.0)
        band = jnp.concatenate([triangle, odd_basis, box_basis], axis=0).astype(bf16)
        start = pl.multiple_of(y * COLS, COLS)
        for a in range(3):
            basis = dot(band, wide[y + a]).astype(bf16)
            for k in range(3):
                pooled[pl.ds(start, COLS), pl.ds((a * 3 + k) * 256, 256)] = basis[
                    k * COLS : (k + 1) * COLS
                ]
        return 0

    lax.fori_loop(0, ROWS, pool, 0)

    whole(s5, g5, 4, 2 * LON - 1).wait_recv()
    far[...] = g5[...].astype(f32).reshape(2 * LON * PAD, HALF)
    matrix = four[...]
    for group in range(6):
        columns = []
        for n in range(8):
            half, row = divmod(group * 8 + n, PAD)
            columns.append(
                jnp.concatenate(
                    trade(
                        far[pl.ds(half * PAD + row, 16, stride=48), :],
                        far[pl.ds((LON + half) * PAD + row, 16, stride=48), :],
                    ),
                    axis=0,
                )
            )
        result = dot(matrix, twice(jnp.concatenate(columns, axis=1).astype(bf16)))
        for n in range(8):
            near[0, pl.ds(group * 8 + n, 32, stride=48), :] = result[
                :, n * HALF : (n + 1) * HALF
            ]
    s6[...] = near[0].reshape(LON, 48, HALF).astype(bf16)
    exchange(s6, g6, 5, ring_peer, lon, LON)

    rows = ROWS * COLS // 4
    for part in range(4):
        convolved[part * rows : (part + 1) * rows, :] = dot(
            pooled[part * rows : (part + 1) * rows, :], conv_weight[...]
        )

    whole(s6, g6, 5, LON - 1).wait_recv()
    far[...] = g6[...].astype(f32).reshape(LON * 48, HALF)

    def finish(y, _):
        spectral = jnp.concatenate(
            [far[pl.ds(half * PAD + y, 32, stride=48), :] for half in range(2)], axis=1
        )
        start = pl.multiple_of(y * COLS, COLS)
        total = convolved[pl.ds(start, COLS), :] + spectral
        gelu = 0.5 * total * (1.0 + lax.erf(total * math.sqrt(0.5)))
        out[y] = (fields[y].astype(f32) + gelu).astype(bf16)
        return 0

    lax.fori_loop(0, ROWS, finish, 0)

    whole(s1, g1, 0, LON - 1).wait_send()
    whole(s2, g2, 1, 2 * LON - 1).wait_send()
    whole(s3, g3, 2, 7).wait_send()
    whole(s4, g4, 3, 7).wait_send()
    whole(s5, g5, 4, 2 * LON - 1).wait_send()
    whole(s6, g6, 5, LON - 1).wait_send()


def per_device(fields, conv_weight, spectral_gain, support):
    vmem = pl.BlockSpec(memory_space=pltpu.VMEM)
    smem = pl.BlockSpec(memory_space=pltpu.SMEM)
    by_ring = pltpu.VMEM((LON, 48, HALF), jnp.bfloat16)
    by_double = pltpu.VMEM((2 * LON, PAD, HALF), jnp.bfloat16)
    by_owner = pltpu.VMEM((8, 192, HALF), jnp.bfloat16)
    tables = longitude_tables() + cycle_tables()
    return pl.pallas_call(
        block_kernel,
        out_shape=jax.ShapeDtypeStruct(fields.shape, fields.dtype),
        in_specs=[vmem, vmem, vmem, smem] + [vmem] * 7,
        out_specs=vmem,
        scratch_shapes=[by_ring] * 2
        + [by_double] * 2
        + [by_owner] * 4
        + [by_double] * 2
        + [by_ring] * 2
        + [
            pltpu.VMEM((ROWS + 2, 3 * COLS, 256), jnp.bfloat16),
            pltpu.VMEM((ROWS * COLS, 9 * 256), jnp.bfloat16),
            pltpu.VMEM((ROWS * COLS, 256), jnp.float32),
            pltpu.VMEM((2, LON * 48, HALF), jnp.float32),
            pltpu.VMEM((LON * 48, HALF), jnp.float32),
            pltpu.VMEM((4 * M, HALF), jnp.float32),
            pltpu.VMEM((4 * M, HALF), jnp.float32),
            pltpu.VMEM((X // HALF, 4 * M, HALF), jnp.float32),
            pltpu.VMEM((4, M, X), jnp.bfloat16),
            pltpu.VMEM((M, HALF), jnp.float32),
            pltpu.SemaphoreType.DMA((10,)),
            pltpu.SemaphoreType.DMA((10,)),
        ],
        compiler_params=pltpu.CompilerParams(
            collective_id=0, has_side_effects=True, vmem_limit_bytes=48 * 2**20
        ),
    )(
        fields, conv_weight.reshape(9 * 256, 256), spectral_gain, support,
        *[jnp.asarray(table) for table in tables],
    )


def solution(mesh):
    placed = (P("lat", "lon", None), P(), P(), P("lat"))
    return jax.shard_map(
        per_device, mesh=mesh, in_specs=placed, out_specs=P("lat", "lon", None), check_vma=False
    )
```

```python
import functools
import math

import jax
import jax.numpy as jnp
import numpy as np
from jax import lax
from jax.experimental import pallas as pl
from jax.experimental.pallas import tpu as pltpu
from jax.sharding import PartitionSpec as P

NLAT = 368
NLON = 1024
M = 512
SMAX = 24
LAT = 16
LON = 32
ROWS = 23
PAD = 24
COLS = 32
HALF = 128
X = LAT * PAD
MESH = pl.DeviceIdType.MESH


def split_pair(table):
    upper_part = table.astype(jnp.bfloat16)
    lower_part = (table - upper_part.astype(jnp.float32)).astype(jnp.bfloat16)
    return upper_part, lower_part


def doubled(table):
    upper = table.astype(jnp.bfloat16)
    lower = (table - upper.astype(np.float32)).astype(jnp.bfloat16)
    return np.concatenate([upper, lower], axis=-1)


def orders_of(bin_index, lat_index):
    first = bin_index + 32 * lat_index
    second = (496 if bin_index == 0 else 512) - first
    return first, second


@functools.lru_cache
def longitude_tables():
    turn = 2.0 * np.pi / NLON
    b = np.arange(32)
    step_one = np.zeros((2, 16, 32))
    for q in range(16):
        step_one[0, q] = np.cos(2 * np.pi * b * q / 32)
        step_one[1, q] = np.sin(2 * np.pi * b * q / 32) if q else (-1.0) ** b
    step_one = step_one.reshape(32, 32)
    r = np.arange(32)
    step_two = np.zeros((16, 2, 2, 16, 2, 32))
    weight = np.zeros((16, 2, 2, 16))
    for q in range(16):
        for a in range(16):
            for u, m in enumerate(orders_of(q, a)):
                cos, sin = np.cos(turn * ((m * r) % NLON)), np.sin(turn * ((m * r) % NLON))
                weight[q, u, :, a] = 1.0 if m == 0 else 2.0
                if q == 0:
                    step_two[q, u, 0, a, u] = cos
                    step_two[q, u, 1, a, u] = sin
                else:
                    sign = 1.0 if u == 0 else -1.0
                    step_two[q, u, 0, a, 0] = cos
                    step_two[q, u, 0, a, 1] = -sign * sin
                    step_two[q, u, 1, a, 0] = sin
                    step_two[q, u, 1, a, 1] = sign * cos
    step_two = step_two.reshape(16, 2, 2, 8, 2, 64).transpose(0, 2, 4, 1, 3, 5).reshape(16, 64, 64)
    weight = weight.reshape(16, 2, 2, 8, 2).transpose(0, 2, 4, 1, 3).reshape(16, 64, 1)
    back = np.swapaxes(step_two * weight, 1, 2)
    f32 = np.float32
    return (
        doubled(step_one.astype(f32)),
        doubled((step_two / NLON).astype(f32)),
        doubled(back.astype(f32)),
        doubled(step_one.T.astype(f32)),
    )


@functools.lru_cache
def cycle_tables():
    t = np.pi * (np.arange(NLAT) + 0.5) / NLAT
    f32 = np.float32

    def placed(values):
        padded = np.zeros((LAT, PAD))
        padded[:, :ROWS] = values.reshape(LAT, ROWS)
        return padded.reshape(4, 2, 2, 3, 8).transpose(3, 0, 2, 1, 4).astype(f32)

    weight = placed(np.sin(t) * np.pi / NLAT).reshape(3, 8, 2, 8).transpose(1, 0, 3, 2)
    weight = np.repeat(weight.reshape(8, PAD, 2), 64, axis=2)
    k = np.arange(1, M)
    log_norm = np.concatenate([[0.0], np.cumsum(np.log((2 * k - 1) / (2 * k)))])
    log_norm = 0.5 * np.log((2 * np.arange(M) + 1) / 2) + 0.5 * log_norm
    rows = np.stack(
        [placed(np.cos(t)).reshape(X), placed(np.log(np.sin(t))).reshape(X), placed(np.ones(NLAT)).reshape(X)]
    )
    return rows, weight, log_norm.reshape(1, M).astype(f32)


def dot(left, right):
    return jnp.dot(left, right, preferred_element_type=jnp.float32)


def twice(block):
    return jnp.concatenate([block, block], axis=0)


def trade(first, second):
    low = lax.broadcasted_iota(jnp.int32, first.shape, 1) < 64
    return (
        jnp.where(low, first, pltpu.roll(second, 64, axis=1)),
        jnp.where(low, pltpu.roll(first, 64, axis=1), second),
    )


def legendre_orders(bin_index, owner, cycle_rows, log_norm, up_table, down_table, table, legendre):
    f32 = jnp.float32

    def order_rows(slot):
        first = bin_index + 64 * owner + 32 * (slot // 2)
        return jnp.where(slot % 2 == 0, first, jnp.where(bin_index == 0, 496, 512) - first)

    def coefficients(block, _):
        row = lax.broadcasted_iota(jnp.int32, (128, HALF), 0)
        degree = (block * 32 + row // 4).astype(f32)
        order = order_rows(row % 4).astype(f32)
        gap, total = degree - order, degree + order
        inside = gap > 0.5
        odd = 2.0 * degree + 1.0
        shared = odd / jnp.where(inside, gap * total, 1.0)
        rise = jnp.sqrt(shared * jnp.maximum(2.0 * degree - 1.0, 0.0))
        fall = jnp.sqrt(
            shared * jnp.maximum((gap - 1.0) * (total - 1.0), 0.0) / jnp.maximum(2.0 * degree - 3.0, 1.0)
        )
        start = pl.multiple_of(block * 128, 128)
        up_table[pl.ds(start, 128), :] = jnp.where(inside, rise, 0.0)
        down_table[pl.ds(start, 128), :] = jnp.where(inside, fall, 0.0)
        return 0

    lax.fori_loop(0, 16, coefficients, 0)
    order = order_rows(lax.broadcasted_iota(jnp.int32, (4, X), 0))
    wide_order = order_rows(lax.broadcasted_iota(jnp.int32, (4, M), 0))
    column = lax.broadcasted_iota(jnp.int32, (4, M), 1)
    norm = jnp.sum(jnp.where(column == wide_order, log_norm[...], 0.0), axis=1, keepdims=True)
    cosines = jnp.broadcast_to(cycle_rows[pl.ds(0, 1), :], (4, X))
    log_start = norm + order.astype(f32) * cycle_rows[pl.ds(1, 1), :]
    start_scale = jnp.minimum(log_start, 0.0)
    diagonal = jnp.exp(log_start - start_scale) * cycle_rows[pl.ds(2, 1), :]

    def spread(rows):
        return jnp.concatenate([rows] * (X // HALF), axis=1)

    def steps(block, state):
        latest, before, log_scale = state
        factor = jnp.exp(log_scale)
        for k in range(4):
            degree = block * 4 + k
            up = spread(up_table[pl.ds(4 * degree, 4), :]) * cosines
            down = spread(down_table[pl.ds(4 * degree, 4), :])
            current = up * latest + (jnp.where(order == degree, diagonal, 0.0) - down * before)
            value = current * factor
            for lane in range(X // HALF):
                table[lane, pl.ds(4 * degree, 4), :] = value[:, lane * HALF : (lane + 1) * HALF]
            latest, before = current, latest
        too_big = jnp.abs(latest) > 2.0**24
        shrink = jnp.where(too_big, 2.0**-24, 1.0)
        log_scale = jnp.where(too_big, log_scale + 24.0 * math.log(2.0), log_scale)
        return latest * shrink, before * shrink, log_scale

    blank = jnp.zeros((4, X), f32)
    lax.fori_loop(0, M // 4, steps, (blank, blank, start_scale))
    for slot in range(4):
        for lane in range(X // HALF):
            legendre[slot, :, lane * HALF : (lane + 1) * HALF] = table[
                lane, pl.ds(slot, M, stride=4), :
            ].astype(jnp.bfloat16)


def block_kernel(
    fields_in, conv_in, gain_in, support_in, one_in, two_in, three_in, four_in, cycles_in,
    weight_in, norm_in,
    out,
    s1, g1, s2, g2, s3, g3, s4, g4, s5, g5, s6, g6, wide, edge_out, edge_in, pooled, convolved,
    near, far, plain,
    up_table, down_table, table, legendre, gains, total,
    cycles, conv_weight, gain, support, one, two, three, four, cycle_rows, weight, log_norm,
    fetch, send, recv, halo_send, halo_recv, ready,
):
    lat = lax.axis_index("lat")
    lon = lax.axis_index("lon")
    hemi = lat // 2 % 2
    owner = lat // 4 * 2 + lat % 2
    spot = hemi * LON + lon
    bin_index, half_index = lon // 2, lon % 2
    f32, bf16 = jnp.float32, jnp.bfloat16

    def double_peer(step):
        index = (spot + step) % (2 * LON)
        return index, (lat // 4 * 4 + index // LON * 2 + lat % 2, index % LON)

    def owner_peer(step):
        index = (owner + step) % 8
        return index, (index // 2 * 4 + hemi * 2 + index % 2, lon)

    def ring_peer(step):
        index = (lon + step) % LON
        return index, (lat, index)

    barrier = pltpu.get_barrier_semaphore()

    def greet(peer_of):
        def one_peer(step, _):
            pl.semaphore_signal(barrier, inc=1, device_id=peer_of(step)[1], device_id_type=MESH)
            return 0

        return one_peer

    partner = (lat // 4 * 4 + (1 - hemi) * 2 + lat % 2, lon)
    lax.fori_loop(1, LON, greet(ring_peer), 0)
    lax.fori_loop(1, 8, greet(owner_peer), 0)
    for device in (((lat + 1) % LAT, lon), ((lat + LAT - 1) % LAT, lon), partner):
        pl.semaphore_signal(barrier, inc=1, device_id=device, device_id_type=MESH)

    own_lanes = pl.ds(pl.multiple_of(half_index * HALF, HALF), HALF)
    sources = [
        (fields_in, cycles.at[pl.ds(1, ROWS)]), (cycles_in, cycle_rows), (norm_in, log_norm), (one_in, one),
        (gain_in.at[:, own_lanes], gain), (two_in.at[bin_index], two),
        (weight_in.at[owner], weight), (three_in.at[bin_index], three), (support_in, support),
        (four_in, four), (conv_in, conv_weight),
    ]
    fetches = [
        pltpu.make_async_copy(source, target, fetch.at[index])
        for index, (source, target) in enumerate(sources)
    ]
    for copy in fetches:
        copy.start()

    ring = (ring_peer, lon, LON)
    double = (double_peer, spot, 2 * LON)
    owners = (owner_peer, owner, 8)
    plan = [
        (s1, g1, ring), (s2, g2, double), (s3, g3, owners),
        (s4, g4, owners), (s5, g5, double), (s6, g6, ring),
    ]

    def exchange(stage, chunk):
        source, target, (peer_of, mine, count) = plan[stage]

        def one_peer(step, _):
            peer, device = peer_of(step)
            pltpu.make_async_remote_copy(
                src_ref=source.at[chunk, peer], dst_ref=target.at[chunk, mine],
                send_sem=send.at[stage, chunk], recv_sem=recv.at[stage, chunk],
                device_id=device, device_id_type=MESH,
            ).start()
            return 0

        lax.fori_loop(1, count, one_peer, 0)
        target[chunk, mine] = source[chunk, mine]

    def whole(stage, chunk):
        source, target, (_, _, count) = plan[stage]
        return pltpu.make_async_remote_copy(
            src_ref=source.at[chunk, pl.ds(0, count - 1)],
            dst_ref=target.at[chunk, pl.ds(0, count - 1)],
            send_sem=send.at[stage, chunk], recv_sem=recv.at[stage, chunk],
            device_id=(lat, (lon + 1) % LON), device_id_type=MESH,
        )

    def arrived(stage, chunk):
        whole(stage, chunk).wait_recv()
        target = plan[stage][1]
        return target[chunk].astype(f32).reshape(512, HALF)

    fetches[0].wait()
    for half in range(2):
        lanes = slice(half * HALF, (half + 1) * HALF)
        plain[half, pl.ds(0, ROWS * COLS), :] = (
            cycles[1 : ROWS + 1, :, lanes].astype(f32).reshape(ROWS * COLS, HALF)
        )
        plain[half, pl.ds(ROWS * COLS, COLS), :] = jnp.zeros((COLS, HALF), f32)

    for chunk in range(3):

        def pack_residue(r, _, chunk=chunk):
            rows = [
                plain[half, pl.ds(chunk * 8 * COLS + r, 8, stride=COLS), :] for half in range(2)
            ]
            s1[chunk, r] = jnp.concatenate(rows, axis=0).astype(bf16)
            return 0

        lax.fori_loop(0, LON, pack_residue, 0)
        if chunk == 0:
            pl.semaphore_wait(barrier, LON - 1 + 7 + 3)
            pl.semaphore_signal(ready, inc=1, device_id=partner, device_id_type=MESH)
        exchange(0, chunk)

    halo_down = pltpu.make_async_remote_copy(
        src_ref=cycles.at[ROWS], dst_ref=cycles.at[0], send_sem=halo_send.at[2],
        recv_sem=halo_recv.at[2], device_id=((lat + 1) % LAT, lon), device_id_type=MESH,
    )
    halo_up = pltpu.make_async_remote_copy(
        src_ref=cycles.at[1], dst_ref=cycles.at[ROWS + 1], send_sem=halo_send.at[3],
        recv_sem=halo_recv.at[3], device_id=((lat + LAT - 1) % LAT, lon), device_id_type=MESH,
    )
    halo_down.start()
    halo_up.start()

    for copy in fetches[1:]:
        copy.wait()
    legendre_orders(
        bin_index, owner, cycle_rows, log_norm, up_table, down_table, table, legendre
    )
    turned = pltpu.roll(gain[...], 64, axis=1)
    lane_half = lax.broadcasted_iota(jnp.int32, (M, HALF), 1) // 64
    gains[...] = jnp.where(lane_half == hemi, gain[...], turned)

    for chunk in range(3):
        far[...] = arrived(0, chunk)
        block = jnp.concatenate(
            [far[pl.ds(n, 32, stride=16), :] for n in range(16)], axis=1
        ).astype(bf16)
        result = dot(one[...], twice(block))
        for n in range(16):
            half, row = divmod(n, 8)
            lanes = slice(n * HALF, (n + 1) * HALF)
            quarters = trade(result[0:16, lanes], result[16:32, lanes])
            for g in range(2):
                near[pl.ds((g * LON + half) * 8 + row, 16, stride=16), :] = quarters[g]
        s2[chunk] = near[...].reshape(2 * LON, 8, HALF).astype(bf16)
        if chunk == 0:
            pl.semaphore_wait(ready, 1)
        exchange(1, chunk)

    halo_down.wait_recv()
    halo_up.wait_recv()
    edge = jnp.full((COLS, 2 * HALF), lat, jnp.int32)
    cycles[0] = jnp.where(edge > 0, cycles[0].astype(f32), 0.0).astype(bf16)
    cycles[ROWS + 1] = jnp.where(edge < LAT - 1, cycles[ROWS + 1].astype(f32), 0.0).astype(bf16)

    def pack_edges(y, _):
        row = cycles[y].astype(f32)
        edge_out[0, y] = row[COLS - SMAX :].astype(bf16)
        edge_out[1, y] = row[:SMAX].astype(bf16)
        return 0

    lax.fori_loop(0, ROWS + 2, pack_edges, 0)
    halo_right = pltpu.make_async_remote_copy(
        src_ref=edge_out.at[0], dst_ref=edge_in.at[0],
        send_sem=halo_send.at[0], recv_sem=halo_recv.at[0],
        device_id=(lat, (lon + 1) % LON), device_id_type=MESH,
    )
    halo_left = pltpu.make_async_remote_copy(
        src_ref=edge_out.at[1], dst_ref=edge_in.at[1],
        send_sem=halo_send.at[1], recv_sem=halo_recv.at[1],
        device_id=(lat, (lon + LON - 1) % LON), device_id_type=MESH,
    )

    for chunk in range(3):
        far[...] = arrived(1, chunk)
        if chunk == 2:
            halo_right.start()
            halo_left.start()
        columns = [
            jnp.concatenate(
                trade(far[pl.ds(row, 32, stride=8), :], far[pl.ds(256 + row, 32, stride=8), :]),
                axis=0,
            )
            for row in range(8)
        ]
        result = dot(two[...], twice(jnp.concatenate(columns, axis=1).astype(bf16)))
        for row in range(8):
            scaled = result[:, row * HALF : (row + 1) * HALF] * weight[pl.ds(chunk * 8 + row, 1), :]
            sides = trade(scaled[0:32], scaled[32:64])
            for g in range(2):
                for slot in range(4):
                    near[pl.ds(slot * 16 + g * 8 + row, 8, stride=64), :] = sides[g][
                        slot * 8 : slot * 8 + 8
                    ]
        s3[chunk] = near[...].reshape(8, 64, HALF).astype(bf16)
        exchange(2, chunk)

    for chunk in range(3):
        whole(2, chunk).wait_recv()
        lanes = slice(chunk * HALF, (chunk + 1) * HALF)
        for slot in range(4):
            data = g3[chunk, :, slot * 16 : slot * 16 + 16, :].reshape(HALF, HALF)
            part = dot(legendre[slot, :, lanes], data)
            if chunk == 0:
                total[slot] = part
            elif chunk == 1:
                total[slot] += part
            else:
                pooled[pl.ds(0, M), pl.ds(slot * HALF, HALF)] = (
                    (total[slot] + part) * gains[...]
                ).astype(bf16)
    for chunk in range(3):
        lanes = slice(chunk * HALF, (chunk + 1) * HALF)
        for slot in range(4):
            synthesis = lax.dot_general(
                legendre[slot, :, lanes],
                pooled[pl.ds(0, M), pl.ds(slot * HALF, HALF)],
                (((0,), (0,)), ((), ())),
                preferred_element_type=f32,
            )
            s4[chunk, :, slot * 16 : slot * 16 + 16, :] = synthesis.reshape(8, 16, HALF).astype(bf16)
        exchange(3, chunk)

    for chunk in range(3):
        far[...] = arrived(3, chunk)
        columns = []
        for row in range(8):
            sides = [
                jnp.concatenate(
                    [far[pl.ds(slot * 16 + g * 8 + row, 8, stride=64), :] for slot in range(4)],
                    axis=0,
                )
                for g in range(2)
            ]
            columns.append(jnp.concatenate(trade(*sides), axis=0))
        result = dot(three[...], twice(jnp.concatenate(columns, axis=1).astype(bf16)))
        for row in range(8):
            lanes = slice(row * HALF, (row + 1) * HALF)
            sides = trade(result[0:32, lanes], result[32:64, lanes])
            for g in range(2):
                near[pl.ds(g * 256 + row, 32, stride=8), :] = sides[g]
        s5[chunk] = near[...].reshape(2 * LON, 8, HALF).astype(bf16)
        exchange(4, chunk)

    halo_right.wait_recv()
    halo_left.wait_recv()

    def widen(y, _):
        sides = [edge_in[0, y], cycles[y], edge_in[1, y]]
        wide[y] = jnp.concatenate([side.astype(f32) for side in sides], axis=0).astype(bf16)
        return 0

    lax.fori_loop(0, ROWS + 2, widen, 0)
    source = lax.broadcasted_iota(jnp.int32, (COLS, COLS + 2 * SMAX), 1)
    target = lax.broadcasted_iota(jnp.int32, (COLS, COLS + 2 * SMAX), 0)
    offset = source - target - SMAX
    offset_real = offset.astype(f32)
    distance = jnp.abs(offset)
    distance_real = distance.astype(f32)

    def pool(y, _):
        half_width = jnp.full((COLS, COLS + 2 * SMAX), support[y], jnp.int32)
        span_len = (half_width + 1).astype(f32)
        inside = distance <= half_width
        triangle = jnp.where(inside, (span_len - distance_real) / span_len, 0.0)
        odd_basis = offset_real * triangle / span_len
        box_basis = jnp.where(inside, 1.0, 0.0) / jnp.sqrt(2.0 * half_width.astype(f32) + 1.0)
        band = jnp.concatenate([triangle, odd_basis, box_basis], axis=0).astype(bf16)
        start = pl.multiple_of(y * COLS, COLS)
        for a in range(3):
            basis = dot(band, wide[y + a]).astype(bf16)
            for k in range(3):
                pooled[pl.ds(start, COLS), pl.ds((a * 3 + k) * 256, 256)] = basis[
                    k * COLS : (k + 1) * COLS
                ]
        return 0

    lax.fori_loop(0, ROWS, pool, 0)

    for chunk in range(3):
        far[...] = arrived(4, chunk)
        columns = [
            jnp.concatenate(
                trade(far[pl.ds(n, 16, stride=16), :], far[pl.ds(256 + n, 16, stride=16), :]), axis=0
            )
            for n in range(16)
        ]
        result = dot(four[...], twice(jnp.concatenate(columns, axis=1).astype(bf16)))
        for n in range(16):
            near[pl.ds(n, 32, stride=16), :] = result[:, n * HALF : (n + 1) * HALF]
        s6[chunk] = near[...].reshape(LON, 16, HALF).astype(bf16)
        exchange(5, chunk)

    rows = ROWS * COLS // 4
    for part in range(4):
        convolved[part * rows : (part + 1) * rows, :] = dot(
            pooled[part * rows : (part + 1) * rows, :], conv_weight[...]
        )

    for chunk in range(3):
        far[...] = arrived(5, chunk)
        for row in range(8 if chunk < 2 else 7):
            y = chunk * 8 + row
            spectral = jnp.concatenate(
                [far[pl.ds(half * 8 + row, 32, stride=16), :] for half in range(2)], axis=1
            )
            branch = convolved[pl.ds(y * COLS, COLS), :] + spectral
            gelu = 0.5 * branch * (1.0 + lax.erf(branch * math.sqrt(0.5)))
            out[y] = (cycles[y + 1].astype(f32) + gelu).astype(bf16)

    for stage in range(6):
        for chunk in range(3):
            whole(stage, chunk).wait_send()
    for copy in (halo_right, halo_left, halo_down, halo_up):
        copy.wait_send()


def per_device(fields, conv_weight, spectral_gain, support):
    vmem = pl.BlockSpec(memory_space=pltpu.VMEM)
    hbm = pl.BlockSpec(memory_space=pltpu.HBM)
    f32, bf16 = jnp.float32, jnp.bfloat16
    by_ring = pltpu.VMEM((3, LON, 16, HALF), bf16)
    by_double = pltpu.VMEM((3, 2 * LON, 8, HALF), bf16)
    by_owner = pltpu.VMEM((3, 8, 64, HALF), bf16)
    tables = longitude_tables() + cycle_tables()
    return pl.pallas_call(
        block_kernel,
        out_shape=jax.ShapeDtypeStruct(fields.shape, fields.dtype),
        in_specs=[hbm] * 11,
        out_specs=vmem,
        scratch_shapes=[by_ring] * 2
        + [by_double] * 2
        + [by_owner] * 4
        + [by_double] * 2
        + [by_ring] * 2
        + [
            pltpu.VMEM((ROWS + 2, COLS + 2 * SMAX, 256), bf16),
            pltpu.VMEM((2, ROWS + 2, SMAX, 256), bf16),
            pltpu.VMEM((2, ROWS + 2, SMAX, 256), bf16),
            pltpu.VMEM((ROWS * COLS, 9 * 256), bf16),
            pltpu.VMEM((ROWS * COLS, 256), f32),
            pltpu.VMEM((512, HALF), f32),
            pltpu.VMEM((512, HALF), f32),
            pltpu.VMEM((2, PAD * COLS, HALF), f32),
            pltpu.VMEM((4 * M, HALF), f32),
            pltpu.VMEM((4 * M, HALF), f32),
            pltpu.VMEM((X // HALF, 4 * M, HALF), f32),
            pltpu.VMEM((4, M, X), bf16),
            pltpu.VMEM((M, HALF), f32),
            pltpu.VMEM((4, M, HALF), f32),
            pltpu.VMEM((ROWS + 2, COLS, 256), bf16),
            pltpu.VMEM((9 * 256, 256), bf16),
            pltpu.VMEM((M, HALF), f32),
            pltpu.SMEM((ROWS,), jnp.int32),
            pltpu.VMEM((32, 64), bf16),
            pltpu.VMEM((64, 128), bf16),
            pltpu.VMEM((64, 128), bf16),
            pltpu.VMEM((32, 64), bf16),
            pltpu.VMEM((3, X), f32),
            pltpu.VMEM((PAD, HALF), f32),
            pltpu.VMEM((1, M), f32),
            pltpu.SemaphoreType.DMA((11,)),
            pltpu.SemaphoreType.DMA((6, 3)),
            pltpu.SemaphoreType.DMA((6, 3)),
            pltpu.SemaphoreType.DMA((4,)),
            pltpu.SemaphoreType.DMA((4,)),
            pltpu.SemaphoreType.REGULAR,
        ],
        compiler_params=pltpu.CompilerParams(
            collective_id=0, has_side_effects=True, vmem_limit_bytes=48 * 2**20
        ),
    )(
        fields, conv_weight.reshape(9 * 256, 256), spectral_gain, support,
        *[jnp.asarray(table) for table in tables],
    )


def solution(mesh):
    placed = (P("lat", "lon", None), P(), P(), P("lat"))
    return jax.shard_map(
        per_device, mesh=mesh, in_specs=placed, out_specs=P("lat", "lon", None), check_vma=False
    )
```

```python
import functools
import math

import jax
import jax.numpy as jnp
import numpy as np
from jax import lax
from jax.experimental import pallas as pl
from jax.experimental.pallas import tpu as pltpu
from jax.sharding import PartitionSpec as P

NLAT = 368
NLON = 1024
M = 512
SMAX = 24
LAT = 16
LON = 32
ROWS = 23
PAD = 24
COLS = 32
HALF = 128
X = LAT * PAD
MESH = pl.DeviceIdType.MESH


def split_pair(table):
    upper_part = table.astype(jnp.bfloat16)
    lower_part = (table - upper_part.astype(jnp.float32)).astype(jnp.bfloat16)
    return upper_part, lower_part


def doubled(table):
    upper = table.astype(jnp.bfloat16)
    lower = (table - upper.astype(np.float32)).astype(jnp.bfloat16)
    return np.concatenate([upper, lower], axis=-1)


def orders_of(bin_index, lat_index):
    first = bin_index + 32 * lat_index
    second = (496 if bin_index == 0 else 512) - first
    return first, second


@functools.lru_cache
def longitude_tables():
    turn = 2.0 * np.pi / NLON
    b = np.arange(32)
    step_one = np.zeros((2, 16, 32))
    for q in range(16):
        step_one[0, q] = np.cos(2 * np.pi * b * q / 32)
        step_one[1, q] = np.sin(2 * np.pi * b * q / 32) if q else (-1.0) ** b
    step_one = step_one.reshape(32, 32)
    r = np.arange(32)
    step_two = np.zeros((16, 2, 2, 16, 2, 32))
    weight = np.zeros((16, 2, 2, 16))
    for q in range(16):
        for a in range(16):
            for u, m in enumerate(orders_of(q, a)):
                cos, sin = np.cos(turn * ((m * r) % NLON)), np.sin(turn * ((m * r) % NLON))
                weight[q, u, :, a] = 1.0 if m == 0 else 2.0
                if q == 0:
                    step_two[q, u, 0, a, u] = cos
                    step_two[q, u, 1, a, u] = sin
                else:
                    sign = 1.0 if u == 0 else -1.0
                    step_two[q, u, 0, a, 0] = cos
                    step_two[q, u, 0, a, 1] = -sign * sin
                    step_two[q, u, 1, a, 0] = sin
                    step_two[q, u, 1, a, 1] = sign * cos
    step_two = step_two.reshape(16, 2, 2, 8, 2, 64).transpose(0, 2, 4, 1, 3, 5).reshape(16, 64, 64)
    weight = weight.reshape(16, 2, 2, 8, 2).transpose(0, 2, 4, 1, 3).reshape(16, 64, 1)
    back = np.swapaxes(step_two * weight, 1, 2)
    f32 = np.float32
    return (
        doubled(step_one.astype(f32)),
        doubled((step_two / NLON).astype(f32)),
        doubled(back.astype(f32)),
        doubled(step_one.T.astype(f32)),
    )


@functools.lru_cache
def cycle_tables():
    t = np.pi * (np.arange(NLAT) + 0.5) / NLAT
    f32 = np.float32

    def placed(values):
        padded = np.zeros((LAT, PAD))
        padded[:, :ROWS] = values.reshape(LAT, ROWS)
        return padded.reshape(4, 2, 2, 3, 8).transpose(3, 0, 2, 1, 4).astype(f32)

    weight = placed(np.sin(t) * np.pi / NLAT).reshape(3, 8, 2, 8).transpose(1, 0, 3, 2)
    weight = np.repeat(weight.reshape(8, PAD, 2), 64, axis=2)
    k = np.arange(1, M)
    log_norm = np.concatenate([[0.0], np.cumsum(np.log((2 * k - 1) / (2 * k)))])
    log_norm = 0.5 * np.log((2 * np.arange(M) + 1) / 2) + 0.5 * log_norm
    rows = np.stack(
        [placed(np.cos(t)).reshape(X), placed(np.log(np.sin(t))).reshape(X), placed(np.ones(NLAT)).reshape(X)]
    )
    return rows, weight, log_norm.reshape(1, M).astype(f32)


def dot(left, right):
    return jnp.dot(left, right, preferred_element_type=jnp.float32)


def twice(block):
    return jnp.concatenate([block, block], axis=0)


def trade(first, second):
    low = lax.broadcasted_iota(jnp.int32, first.shape, 1) < 64
    return (
        jnp.where(low, first, pltpu.roll(second, 64, axis=1)),
        jnp.where(low, pltpu.roll(first, 64, axis=1), second),
    )


def legendre_orders(bin_index, owner, cycle_rows, log_norm, up_table, down_table, table, legendre):
    f32 = jnp.float32

    def order_rows(slot):
        first = bin_index + 64 * owner + 32 * (slot // 2)
        return jnp.where(slot % 2 == 0, first, jnp.where(bin_index == 0, 496, 512) - first)

    def coefficients(block, _):
        row = lax.broadcasted_iota(jnp.int32, (128, HALF), 0)
        degree = (block * 32 + row // 4).astype(f32)
        order = order_rows(row % 4).astype(f32)
        gap, total = degree - order, degree + order
        inside = gap > 0.5
        odd = 2.0 * degree + 1.0
        shared = odd / jnp.where(inside, gap * total, 1.0)
        rise = jnp.sqrt(shared * jnp.maximum(2.0 * degree - 1.0, 0.0))
        fall = jnp.sqrt(
            shared * jnp.maximum((gap - 1.0) * (total - 1.0), 0.0) / jnp.maximum(2.0 * degree - 3.0, 1.0)
        )
        start = pl.multiple_of(block * 128, 128)
        up_table[pl.ds(start, 128), :] = jnp.where(inside, rise, 0.0)
        down_table[pl.ds(start, 128), :] = jnp.where(inside, fall, 0.0)
        return 0

    lax.fori_loop(0, 16, coefficients, 0)
    order = order_rows(lax.broadcasted_iota(jnp.int32, (4, X), 0))
    wide_order = order_rows(lax.broadcasted_iota(jnp.int32, (4, M), 0))
    column = lax.broadcasted_iota(jnp.int32, (4, M), 1)
    norm = jnp.sum(jnp.where(column == wide_order, log_norm[...], 0.0), axis=1, keepdims=True)
    cosines = jnp.broadcast_to(cycle_rows[pl.ds(0, 1), :], (4, X))
    log_start = norm + order.astype(f32) * cycle_rows[pl.ds(1, 1), :]
    start_scale = jnp.minimum(log_start, 0.0)
    diagonal = jnp.exp(log_start - start_scale) * cycle_rows[pl.ds(2, 1), :]

    def spread(rows):
        return jnp.concatenate([rows] * (X // HALF), axis=1)

    def steps(block, state):
        latest, before, log_scale = state
        factor = jnp.exp(log_scale)
        for k in range(4):
            degree = block * 4 + k
            up = spread(up_table[pl.ds(4 * degree, 4), :]) * cosines
            down = spread(down_table[pl.ds(4 * degree, 4), :])
            current = up * latest + (jnp.where(order == degree, diagonal, 0.0) - down * before)
            value = current * factor
            for lane in range(X // HALF):
                table[lane, pl.ds(4 * degree, 4), :] = value[:, lane * HALF : (lane + 1) * HALF]
            latest, before = current, latest
        too_big = jnp.abs(latest) > 2.0**24
        shrink = jnp.where(too_big, 2.0**-24, 1.0)
        log_scale = jnp.where(too_big, log_scale + 24.0 * math.log(2.0), log_scale)
        return latest * shrink, before * shrink, log_scale

    blank = jnp.zeros((4, X), f32)
    lax.fori_loop(0, M // 4, steps, (blank, blank, start_scale))
    for slot in range(4):
        for lane in range(X // HALF):
            legendre[slot, :, lane * HALF : (lane + 1) * HALF] = table[
                lane, pl.ds(slot, M, stride=4), :
            ].astype(jnp.bfloat16)


def block_kernel(
    fields_in, conv_in, gain_in, support_in, one_in, two_in, three_in, four_in, cycles_in,
    weight_in, norm_in,
    out,
    s1, g1, s2, g2, s3, g3, s4, g4, s5, g5, s6, g6, wide, edge_out, edge_in, pooled, convolved,
    near, far, plain,
    up_table, down_table, table, legendre, gains, total,
    cycles, conv_weight, gain, support, one, two, three, four, cycle_rows, weight, log_norm,
    fetch, send, recv, halo_send, halo_recv, ready,
):
    lat = lax.axis_index("lat")
    lon = lax.axis_index("lon")
    hemi = lat // 2 % 2
    owner = lat // 4 * 2 + lat % 2
    spot = hemi * LON + lon
    bin_index, half_index = lon // 2, lon % 2
    f32, bf16 = jnp.float32, jnp.bfloat16

    def double_peer(step):
        index = (spot + step) % (2 * LON)
        return index, (lat // 4 * 4 + index // LON * 2 + lat % 2, index % LON)

    def owner_peer(step):
        index = (owner + step) % 8
        return index, (index // 2 * 4 + hemi * 2 + index % 2, lon)

    def ring_peer(step):
        index = (lon + step) % LON
        return index, (lat, index)

    barrier = pltpu.get_barrier_semaphore()

    def greet(peer_of):
        def one_peer(step, _):
            pl.semaphore_signal(barrier, inc=1, device_id=peer_of(step)[1], device_id_type=MESH)
            return 0

        return one_peer

    partner = (lat // 4 * 4 + (1 - hemi) * 2 + lat % 2, lon)
    lax.fori_loop(1, LON, greet(ring_peer), 0)
    lax.fori_loop(1, 8, greet(owner_peer), 0)
    for device in (((lat + 1) % LAT, lon), ((lat + LAT - 1) % LAT, lon), partner):
        pl.semaphore_signal(barrier, inc=1, device_id=device, device_id_type=MESH)

    own_lanes = pl.ds(pl.multiple_of(half_index * HALF, HALF), HALF)
    sources = [
        (fields_in, cycles.at[pl.ds(1, ROWS)]), (cycles_in, cycle_rows), (norm_in, log_norm), (one_in, one),
        (gain_in.at[:, own_lanes], gain), (two_in.at[bin_index], two),
        (weight_in.at[owner], weight), (three_in.at[bin_index], three), (support_in, support),
        (four_in, four), (conv_in, conv_weight),
    ]
    fetches = [
        pltpu.make_async_copy(source, target, fetch.at[index])
        for index, (source, target) in enumerate(sources)
    ]
    for copy in fetches:
        copy.start()

    ring = (ring_peer, lon, LON)
    double = (double_peer, spot, 2 * LON)
    owners = (owner_peer, owner, 8)
    plan = [
        (s1, g1, ring), (s2, g2, double), (s3, g3, owners),
        (s4, g4, owners), (s5, g5, double), (s6, g6, ring),
    ]

    def exchange(stage, chunk):
        source, target, (peer_of, mine, count) = plan[stage]

        def one_peer(step, _):
            peer, device = peer_of(step)
            pltpu.make_async_remote_copy(
                src_ref=source.at[chunk, peer], dst_ref=target.at[chunk, mine],
                send_sem=send.at[stage, chunk], recv_sem=recv.at[stage, chunk],
                device_id=device, device_id_type=MESH,
            ).start()
            return 0

        lax.fori_loop(1, count, one_peer, 0)
        target[chunk, mine] = source[chunk, mine]

    def whole(stage, chunk):
        source, target, (_, _, count) = plan[stage]
        return pltpu.make_async_remote_copy(
            src_ref=source.at[chunk, pl.ds(0, count - 1)],
            dst_ref=target.at[chunk, pl.ds(0, count - 1)],
            send_sem=send.at[stage, chunk], recv_sem=recv.at[stage, chunk],
            device_id=(lat, (lon + 1) % LON), device_id_type=MESH,
        )

    def arrived(stage, chunk):
        whole(stage, chunk).wait_recv()
        target = plan[stage][1]
        return target[chunk].astype(f32).reshape(512, HALF)

    fetches[0].wait()
    for half in range(2):
        lanes = slice(half * HALF, (half + 1) * HALF)
        plain[half, pl.ds(0, ROWS * COLS), :] = (
            cycles[1 : ROWS + 1, :, lanes].astype(f32).reshape(ROWS * COLS, HALF)
        )
        plain[half, pl.ds(ROWS * COLS, COLS), :] = jnp.zeros((COLS, HALF), f32)

    for chunk in range(3):

        def pack_residue(r, _, chunk=chunk):
            rows = [
                plain[half, pl.ds(chunk * 8 * COLS + r, 8, stride=COLS), :] for half in range(2)
            ]
            s1[chunk, r] = jnp.concatenate(rows, axis=0).astype(bf16)
            return 0

        lax.fori_loop(0, LON, pack_residue, 0)
        if chunk == 0:
            pl.semaphore_wait(barrier, LON - 1 + 7 + 3)
            pl.semaphore_signal(ready, inc=1, device_id=partner, device_id_type=MESH)
        exchange(0, chunk)

    halo_down = pltpu.make_async_remote_copy(
        src_ref=cycles.at[ROWS], dst_ref=cycles.at[0], send_sem=halo_send.at[2],
        recv_sem=halo_recv.at[2], device_id=((lat + 1) % LAT, lon), device_id_type=MESH,
    )
    halo_up = pltpu.make_async_remote_copy(
        src_ref=cycles.at[1], dst_ref=cycles.at[ROWS + 1], send_sem=halo_send.at[3],
        recv_sem=halo_recv.at[3], device_id=((lat + LAT - 1) % LAT, lon), device_id_type=MESH,
    )
    halo_down.start()
    halo_up.start()

    for copy in fetches[1:]:
        copy.wait()
    legendre_orders(
        bin_index, owner, cycle_rows, log_norm, up_table, down_table, table, legendre
    )
    turned = pltpu.roll(gain[...], 64, axis=1)
    lane_half = lax.broadcasted_iota(jnp.int32, (M, HALF), 1) // 64
    gains[...] = jnp.where(lane_half == hemi, gain[...], turned)

    for chunk in range(3):
        far[...] = arrived(0, chunk)
        block = jnp.concatenate(
            [far[pl.ds(n, 32, stride=16), :] for n in range(16)], axis=1
        ).astype(bf16)
        result = dot(one[...], twice(block))
        for n in range(16):
            half, row = divmod(n, 8)
            lanes = slice(n * HALF, (n + 1) * HALF)
            quarters = trade(result[0:16, lanes], result[16:32, lanes])
            for g in range(2):
                near[pl.ds((g * LON + half) * 8 + row, 16, stride=16), :] = quarters[g]
        s2[chunk] = near[...].reshape(2 * LON, 8, HALF).astype(bf16)
        if chunk == 0:
            pl.semaphore_wait(ready, 1)
        exchange(1, chunk)

    halo_down.wait_recv()
    halo_up.wait_recv()
    edge = jnp.full((COLS, 2 * HALF), lat, jnp.int32)
    cycles[0] = jnp.where(edge > 0, cycles[0].astype(f32), 0.0).astype(bf16)
    cycles[ROWS + 1] = jnp.where(edge < LAT - 1, cycles[ROWS + 1].astype(f32), 0.0).astype(bf16)

    def pack_edges(y, _):
        row = cycles[y].astype(f32)
        edge_out[0, y] = row[COLS - SMAX :].astype(bf16)
        edge_out[1, y] = row[:SMAX].astype(bf16)
        return 0

    lax.fori_loop(0, ROWS + 2, pack_edges, 0)
    halo_right = pltpu.make_async_remote_copy(
        src_ref=edge_out.at[0], dst_ref=edge_in.at[0],
        send_sem=halo_send.at[0], recv_sem=halo_recv.at[0],
        device_id=(lat, (lon + 1) % LON), device_id_type=MESH,
    )
    halo_left = pltpu.make_async_remote_copy(
        src_ref=edge_out.at[1], dst_ref=edge_in.at[1],
        send_sem=halo_send.at[1], recv_sem=halo_recv.at[1],
        device_id=(lat, (lon + LON - 1) % LON), device_id_type=MESH,
    )

    for chunk in range(3):
        far[...] = arrived(1, chunk)
        if chunk == 2:
            halo_right.start()
            halo_left.start()
        columns = [
            jnp.concatenate(
                trade(far[pl.ds(row, 32, stride=8), :], far[pl.ds(256 + row, 32, stride=8), :]),
                axis=0,
            )
            for row in range(8)
        ]
        result = dot(two[...], twice(jnp.concatenate(columns, axis=1).astype(bf16)))
        for row in range(8):
            scaled = result[:, row * HALF : (row + 1) * HALF] * weight[pl.ds(chunk * 8 + row, 1), :]
            sides = trade(scaled[0:32], scaled[32:64])
            for g in range(2):
                for slot in range(4):
                    near[pl.ds(slot * 16 + g * 8 + row, 8, stride=64), :] = sides[g][
                        slot * 8 : slot * 8 + 8
                    ]
        s3[chunk] = near[...].reshape(8, 64, HALF).astype(bf16)
        exchange(2, chunk)

    for chunk in range(3):
        whole(2, chunk).wait_recv()
        lanes = slice(chunk * HALF, (chunk + 1) * HALF)
        for slot in range(4):
            data = g3[chunk, :, slot * 16 : slot * 16 + 16, :].reshape(HALF, HALF)
            part = dot(legendre[slot, :, lanes], data)
            if chunk == 0:
                total[slot] = part
            elif chunk == 1:
                total[slot] += part
            else:
                pooled[pl.ds(0, M), pl.ds(slot * HALF, HALF)] = (
                    (total[slot] + part) * gains[...]
                ).astype(bf16)
    for chunk in range(3):
        lanes = slice(chunk * HALF, (chunk + 1) * HALF)
        for slot in range(4):
            synthesis = lax.dot_general(
                legendre[slot, :, lanes],
                pooled[pl.ds(0, M), pl.ds(slot * HALF, HALF)],
                (((0,), (0,)), ((), ())),
                preferred_element_type=f32,
            )
            s4[chunk, :, slot * 16 : slot * 16 + 16, :] = synthesis.reshape(8, 16, HALF).astype(bf16)
        exchange(3, chunk)

    for chunk in range(3):
        far[...] = arrived(3, chunk)
        columns = []
        for row in range(8):
            sides = [
                jnp.concatenate(
                    [far[pl.ds(slot * 16 + g * 8 + row, 8, stride=64), :] for slot in range(4)],
                    axis=0,
                )
                for g in range(2)
            ]
            columns.append(jnp.concatenate(trade(*sides), axis=0))
        result = dot(three[...], twice(jnp.concatenate(columns, axis=1).astype(bf16)))
        for row in range(8):
            lanes = slice(row * HALF, (row + 1) * HALF)
            sides = trade(result[0:32, lanes], result[32:64, lanes])
            for g in range(2):
                near[pl.ds(g * 256 + row, 32, stride=8), :] = sides[g]
        s5[chunk] = near[...].reshape(2 * LON, 8, HALF).astype(bf16)
        exchange(4, chunk)

    halo_right.wait_recv()
    halo_left.wait_recv()

    def widen(y, _):
        sides = [edge_in[0, y], cycles[y], edge_in[1, y]]
        wide[y] = jnp.concatenate([side.astype(f32) for side in sides], axis=0).astype(bf16)
        return 0

    lax.fori_loop(0, ROWS + 2, widen, 0)
    source = lax.broadcasted_iota(jnp.int32, (COLS, COLS + 2 * SMAX), 1)
    target = lax.broadcasted_iota(jnp.int32, (COLS, COLS + 2 * SMAX), 0)
    offset = source - target - SMAX
    offset_real = offset.astype(f32)
    distance = jnp.abs(offset)
    distance_real = distance.astype(f32)

    def pool(y, _):
        half_width = jnp.full((COLS, COLS + 2 * SMAX), support[y], jnp.int32)
        span_len = (half_width + 1).astype(f32)
        inside = distance <= half_width
        triangle = jnp.where(inside, (span_len - distance_real) / span_len, 0.0)
        odd_basis = offset_real * triangle / span_len
        box_basis = jnp.where(inside, 1.0, 0.0) / jnp.sqrt(2.0 * half_width.astype(f32) + 1.0)
        band = jnp.concatenate([triangle, odd_basis, box_basis], axis=0).astype(bf16)
        start = pl.multiple_of(y * COLS, COLS)
        for a in range(3):
            basis = dot(band, wide[y + a]).astype(bf16)
            for k in range(3):
                pooled[pl.ds(start, COLS), pl.ds((a * 3 + k) * 256, 256)] = basis[
                    k * COLS : (k + 1) * COLS
                ]
        return 0

    lax.fori_loop(0, ROWS, pool, 0)

    for chunk in range(3):
        far[...] = arrived(4, chunk)
        columns = [
            jnp.concatenate(
                trade(far[pl.ds(n, 16, stride=16), :], far[pl.ds(256 + n, 16, stride=16), :]), axis=0
            )
            for n in range(16)
        ]
        result = dot(four[...], twice(jnp.concatenate(columns, axis=1).astype(bf16)))
        for n in range(16):
            near[pl.ds(n, 32, stride=16), :] = result[:, n * HALF : (n + 1) * HALF]
        s6[chunk] = near[...].reshape(LON, 16, HALF).astype(bf16)
        exchange(5, chunk)

    rows = ROWS * COLS // 4
    for part in range(4):
        convolved[part * rows : (part + 1) * rows, :] = dot(
            pooled[part * rows : (part + 1) * rows, :], conv_weight[...]
        )

    for chunk in range(3):
        far[...] = arrived(5, chunk)
        for row in range(8 if chunk < 2 else 7):
            y = chunk * 8 + row
            spectral = jnp.concatenate(
                [far[pl.ds(half * 8 + row, 32, stride=16), :] for half in range(2)], axis=1
            )
            branch = convolved[pl.ds(y * COLS, COLS), :] + spectral
            gelu = 0.5 * branch * (1.0 + lax.erf(branch * math.sqrt(0.5)))
            out[y] = (cycles[y + 1].astype(f32) + gelu).astype(bf16)

    for stage in range(6):
        for chunk in range(3):
            whole(stage, chunk).wait_send()
    for copy in (halo_right, halo_left, halo_down, halo_up):
        copy.wait_send()


def per_device(fields, conv_weight, spectral_gain, support):
    vmem = pl.BlockSpec(memory_space=pltpu.VMEM)
    hbm = pl.BlockSpec(memory_space=pltpu.HBM)
    f32, bf16 = jnp.float32, jnp.bfloat16
    by_ring = pltpu.VMEM((3, LON, 16, HALF), bf16)
    by_double = pltpu.VMEM((3, 2 * LON, 8, HALF), bf16)
    by_owner = pltpu.VMEM((3, 8, 64, HALF), bf16)
    tables = longitude_tables() + cycle_tables()
    return pl.pallas_call(
        block_kernel,
        out_shape=jax.ShapeDtypeStruct(fields.shape, fields.dtype),
        in_specs=[hbm] * 11,
        out_specs=vmem,
        scratch_shapes=[by_ring] * 2
        + [by_double] * 2
        + [by_owner] * 4
        + [by_double] * 2
        + [by_ring] * 2
        + [
            pltpu.VMEM((ROWS + 2, COLS + 2 * SMAX, 256), bf16),
            pltpu.VMEM((2, ROWS + 2, SMAX, 256), bf16),
            pltpu.VMEM((2, ROWS + 2, SMAX, 256), bf16),
            pltpu.VMEM((ROWS * COLS, 9 * 256), bf16),
            pltpu.VMEM((ROWS * COLS, 256), f32),
            pltpu.VMEM((512, HALF), f32),
            pltpu.VMEM((512, HALF), f32),
            pltpu.VMEM((2, PAD * COLS, HALF), f32),
            pltpu.VMEM((4 * M, HALF), f32),
            pltpu.VMEM((4 * M, HALF), f32),
            pltpu.VMEM((X // HALF, 4 * M, HALF), f32),
            pltpu.VMEM((4, M, X), bf16),
            pltpu.VMEM((M, HALF), f32),
            pltpu.VMEM((4, M, HALF), f32),
            pltpu.VMEM((ROWS + 2, COLS, 256), bf16),
            pltpu.VMEM((9 * 256, 256), bf16),
            pltpu.VMEM((M, HALF), f32),
            pltpu.SMEM((ROWS,), jnp.int32),
            pltpu.VMEM((32, 64), bf16),
            pltpu.VMEM((64, 128), bf16),
            pltpu.VMEM((64, 128), bf16),
            pltpu.VMEM((32, 64), bf16),
            pltpu.VMEM((3, X), f32),
            pltpu.VMEM((PAD, HALF), f32),
            pltpu.VMEM((1, M), f32),
            pltpu.SemaphoreType.DMA((11,)),
            pltpu.SemaphoreType.DMA((6, 3)),
            pltpu.SemaphoreType.DMA((6, 3)),
            pltpu.SemaphoreType.DMA((4,)),
            pltpu.SemaphoreType.DMA((4,)),
            pltpu.SemaphoreType.REGULAR,
        ],
        compiler_params=pltpu.CompilerParams(
            collective_id=0, has_side_effects=True, vmem_limit_bytes=64 * 2**20
        ),
    )(
        fields, conv_weight.reshape(9 * 256, 256), spectral_gain, support,
        *[jnp.asarray(table) for table in tables],
    )


def solution(mesh):
    placed = (P("lat", "lon", None), P(), P(), P("lat"))
    return jax.shard_map(
        per_device, mesh=mesh, in_specs=placed, out_specs=P("lat", "lon", None), check_vma=False
    )
```

```python
import functools
import math

import jax
import jax.numpy as jnp
import numpy as np
from jax import lax
from jax.experimental import pallas as pl
from jax.experimental.pallas import tpu as pltpu
from jax.sharding import PartitionSpec as P

NLAT = 368
NLON = 1024
M = 512
SMAX = 24
LAT = 16
LON = 32
ROWS = 23
PAD = 24
COLS = 32
HALF = 128
X = LAT * PAD
MESH = pl.DeviceIdType.MESH


def split_pair(table):
    upper_part = table.astype(jnp.bfloat16)
    lower_part = (table - upper_part.astype(jnp.float32)).astype(jnp.bfloat16)
    return upper_part, lower_part


def doubled(table):
    upper = table.astype(jnp.bfloat16)
    lower = (table - upper.astype(np.float32)).astype(jnp.bfloat16)
    return np.concatenate([upper, lower], axis=-1)


def orders_of(bin_index, lat_index):
    first = bin_index + 32 * lat_index
    second = (496 if bin_index == 0 else 512) - first
    return first, second


@functools.lru_cache
def longitude_tables():
    turn = 2.0 * np.pi / NLON
    b = np.arange(32)
    step_one = np.zeros((2, 16, 32))
    for q in range(16):
        step_one[0, q] = np.cos(2 * np.pi * b * q / 32)
        step_one[1, q] = np.sin(2 * np.pi * b * q / 32) if q else (-1.0) ** b
    step_one = step_one.reshape(32, 32)
    r = np.arange(32)
    step_two = np.zeros((16, 2, 2, 16, 2, 32))
    weight = np.zeros((16, 2, 2, 16))
    for q in range(16):
        for a in range(16):
            for u, m in enumerate(orders_of(q, a)):
                cos, sin = np.cos(turn * ((m * r) % NLON)), np.sin(turn * ((m * r) % NLON))
                weight[q, u, :, a] = 1.0 if m == 0 else 2.0
                if q == 0:
                    step_two[q, u, 0, a, u] = cos
                    step_two[q, u, 1, a, u] = sin
                else:
                    sign = 1.0 if u == 0 else -1.0
                    step_two[q, u, 0, a, 0] = cos
                    step_two[q, u, 0, a, 1] = -sign * sin
                    step_two[q, u, 1, a, 0] = sin
                    step_two[q, u, 1, a, 1] = sign * cos
    step_two = step_two.reshape(16, 2, 2, 8, 2, 64).transpose(0, 2, 4, 1, 3, 5).reshape(16, 64, 64)
    weight = weight.reshape(16, 2, 2, 8, 2).transpose(0, 2, 4, 1, 3).reshape(16, 64, 1)
    back = np.swapaxes(step_two * weight, 1, 2)
    f32 = np.float32
    return (
        doubled(step_one.astype(f32)),
        doubled((step_two / NLON).astype(f32)),
        doubled(back.astype(f32)),
        doubled(step_one.T.astype(f32)),
    )


@functools.lru_cache
def cycle_tables():
    t = np.pi * (np.arange(NLAT) + 0.5) / NLAT
    f32 = np.float32

    def placed(values):
        padded = np.zeros((LAT, PAD))
        padded[:, :ROWS] = values.reshape(LAT, ROWS)
        return padded.reshape(4, 2, 2, 3, 8).transpose(3, 0, 2, 1, 4).astype(f32)

    weight = placed(np.sin(t) * np.pi / NLAT).reshape(3, 8, 2, 8).transpose(1, 0, 3, 2)
    weight = np.repeat(weight.reshape(8, PAD, 2), 64, axis=2)
    k = np.arange(1, M)
    log_norm = np.concatenate([[0.0], np.cumsum(np.log((2 * k - 1) / (2 * k)))])
    log_norm = 0.5 * np.log((2 * np.arange(M) + 1) / 2) + 0.5 * log_norm
    rows = np.stack(
        [placed(np.cos(t)).reshape(X), placed(np.log(np.sin(t))).reshape(X), placed(np.ones(NLAT)).reshape(X)]
    )
    return rows, weight, log_norm.reshape(1, M).astype(f32)


def dot(left, right):
    return jnp.dot(left, right, preferred_element_type=jnp.float32)


def twice(block):
    return jnp.concatenate([block, block], axis=0)


def trade(first, second):
    low = lax.broadcasted_iota(jnp.int32, first.shape, 1) < 64
    return (
        jnp.where(low, first, pltpu.roll(second, 64, axis=1)),
        jnp.where(low, pltpu.roll(first, 64, axis=1), second),
    )


def legendre_orders(bin_index, owner, cycle_rows, log_norm, up_table, down_table, table, legendre):
    f32 = jnp.float32

    def order_rows(slot):
        first = bin_index + 64 * owner + 32 * (slot // 2)
        return jnp.where(slot % 2 == 0, first, jnp.where(bin_index == 0, 496, 512) - first)

    def coefficients(block, _):
        row = lax.broadcasted_iota(jnp.int32, (128, HALF), 0)
        degree = (block * 32 + row // 4).astype(f32)
        order = order_rows(row % 4).astype(f32)
        gap, total = degree - order, degree + order
        inside = gap > 0.5
        odd = 2.0 * degree + 1.0
        shared = odd / jnp.where(inside, gap * total, 1.0)
        rise = jnp.sqrt(shared * jnp.maximum(2.0 * degree - 1.0, 0.0))
        fall = jnp.sqrt(
            shared * jnp.maximum((gap - 1.0) * (total - 1.0), 0.0) / jnp.maximum(2.0 * degree - 3.0, 1.0)
        )
        start = pl.multiple_of(block * 128, 128)
        up_table[pl.ds(start, 128), :] = jnp.where(inside, rise, 0.0)
        down_table[pl.ds(start, 128), :] = jnp.where(inside, fall, 0.0)
        return 0

    lax.fori_loop(0, 16, coefficients, 0)
    order = order_rows(lax.broadcasted_iota(jnp.int32, (4, X), 0))
    wide_order = order_rows(lax.broadcasted_iota(jnp.int32, (4, M), 0))
    column = lax.broadcasted_iota(jnp.int32, (4, M), 1)
    norm = jnp.sum(jnp.where(column == wide_order, log_norm[...], 0.0), axis=1, keepdims=True)
    cosines = jnp.broadcast_to(cycle_rows[pl.ds(0, 1), :], (4, X))
    log_start = norm + order.astype(f32) * cycle_rows[pl.ds(1, 1), :]
    start_scale = jnp.minimum(log_start, 0.0)
    diagonal = jnp.exp(log_start - start_scale) * cycle_rows[pl.ds(2, 1), :]

    def spread(rows):
        return jnp.concatenate([rows] * (X // HALF), axis=1)

    def steps(block, state):
        latest, before, log_scale = state
        factor = jnp.exp(log_scale)
        for k in range(4):
            degree = block * 4 + k
            up = spread(up_table[pl.ds(4 * degree, 4), :]) * cosines
            down = spread(down_table[pl.ds(4 * degree, 4), :])
            current = up * latest + (jnp.where(order == degree, diagonal, 0.0) - down * before)
            value = current * factor
            for lane in range(X // HALF):
                table[lane, pl.ds(4 * degree, 4), :] = value[:, lane * HALF : (lane + 1) * HALF]
            latest, before = current, latest
        too_big = jnp.abs(latest) > 2.0**24
        shrink = jnp.where(too_big, 2.0**-24, 1.0)
        log_scale = jnp.where(too_big, log_scale + 24.0 * math.log(2.0), log_scale)
        return latest * shrink, before * shrink, log_scale

    blank = jnp.zeros((4, X), f32)
    state = lax.fori_loop(0, M // 8, steps, (blank, blank, start_scale))
    yield
    lax.fori_loop(M // 8, M // 4, steps, state)
    for slot in range(4):
        for lane in range(X // HALF):
            legendre[slot, :, lane * HALF : (lane + 1) * HALF] = table[
                lane, pl.ds(slot, M, stride=4), :
            ].astype(jnp.bfloat16)
    yield


def block_kernel(
    fields_in, conv_in, gain_in, support_in, one_in, two_in, three_in, four_in, cycles_in,
    weight_in, norm_in,
    out,
    s1, g1, s2, g2, s3, g3, s4, g4, s5, g5, s6, g6, wide, edge_out, edge_in, pooled, convolved,
    near, far, plain,
    up_table, down_table, table, legendre, gains, total,
    cycles, conv_weight, gain, support, one, two, three, four, cycle_rows, weight, log_norm,
    fetch, send, recv, halo_send, halo_recv, ready,
):
    lat = lax.axis_index("lat")
    lon = lax.axis_index("lon")
    hemi = lat // 2 % 2
    owner = lat // 4 * 2 + lat % 2
    spot = hemi * LON + lon
    double_base = lat // 4 * 4 + lat % 2
    bin_index, half_index = lon // 2, lon % 2
    f32, bf16 = jnp.float32, jnp.bfloat16

    own_lanes = pl.ds(pl.multiple_of(half_index * HALF, HALF), HALF)
    sources = [
        (fields_in, cycles.at[pl.ds(1, ROWS)]), (cycles_in, cycle_rows), (norm_in, log_norm), (one_in, one),
        (gain_in.at[:, own_lanes], gain), (two_in.at[bin_index], two),
        (weight_in.at[owner], weight), (three_in.at[bin_index], three), (support_in, support),
        (four_in, four), (conv_in, conv_weight),
    ]
    fetches = [
        pltpu.make_async_copy(source, target, fetch.at[index])
        for index, (source, target) in enumerate(sources)
    ]
    fetches[0].start()

    def double_peer(step):
        index = lax.rem(spot + step, 2 * LON)
        return index, (double_base + lax.div(index, LON) * 2, lax.rem(index, LON))

    def owner_peer(step):
        index = lax.rem(owner + step, 8)
        return index, (lax.div(index, 2) * 4 + hemi * 2 + lax.rem(index, 2), lon)

    def ring_peer(step):
        index = lax.rem(lon + step, LON)
        return index, (lat, index)

    barrier = pltpu.get_barrier_semaphore()

    def greet(peer_of):
        def one_peer(step, _):
            pl.semaphore_signal(barrier, inc=1, device_id=peer_of(step)[1], device_id_type=MESH)
            return 0

        return one_peer

    partner = (lat // 4 * 4 + (1 - hemi) * 2 + lat % 2, lon)
    lax.fori_loop(1, LON, greet(ring_peer), 0)
    lax.fori_loop(1, 8, greet(owner_peer), 0)
    for device in (((lat + 1) % LAT, lon), ((lat + LAT - 1) % LAT, lon), partner):
        pl.semaphore_signal(barrier, inc=1, device_id=device, device_id_type=MESH)
    for copy in fetches[1:]:
        copy.start()

    ring = (ring_peer, lon, LON)
    double = (double_peer, spot, 2 * LON)
    owners = (owner_peer, owner, 8)
    plan = [
        (s1, g1, ring), (s2, g2, double), (s3, g3, owners),
        (s4, g4, owners), (s5, g5, double), (s6, g6, ring),
    ]

    def exchange(stage, chunk):
        source, target, (peer_of, mine, count) = plan[stage]

        def one_peer(step, _):
            peer, device = peer_of(step)
            pltpu.make_async_remote_copy(
                src_ref=source.at[chunk, peer], dst_ref=target.at[chunk, mine],
                send_sem=send.at[stage, chunk], recv_sem=recv.at[stage, chunk],
                device_id=device, device_id_type=MESH,
            ).start()
            return 0

        lax.fori_loop(1, count, one_peer, 0)
        target[chunk, mine] = source[chunk, mine]

    def whole(stage, chunk):
        source, target, (_, _, count) = plan[stage]
        return pltpu.make_async_remote_copy(
            src_ref=source.at[chunk, pl.ds(0, count - 1)],
            dst_ref=target.at[chunk, pl.ds(0, count - 1)],
            send_sem=send.at[stage, chunk], recv_sem=recv.at[stage, chunk],
            device_id=(lat, (lon + 1) % LON), device_id_type=MESH,
        )

    def arrived(stage, chunk):
        whole(stage, chunk).wait_recv()
        target = plan[stage][1]
        return target[chunk].astype(f32).reshape(512, HALF)

    fetches[0].wait()
    for chunk in range(3):
        count = min(8, ROWS - chunk * 8)
        for half in range(2):
            lanes = slice(half * HALF, (half + 1) * HALF)
            plain[half, pl.ds(chunk * 8 * COLS, count * COLS), :] = (
                cycles[chunk * 8 + 1 : chunk * 8 + 1 + count, :, lanes]
                .astype(f32)
                .reshape(count * COLS, HALF)
            )
            if count < 8:
                plain[half, pl.ds(ROWS * COLS, COLS), :] = jnp.zeros((COLS, HALF), f32)

        def pack_residue(r, _, chunk=chunk):
            rows = [
                plain[half, pl.ds(chunk * 8 * COLS + r, 8, stride=COLS), :] for half in range(2)
            ]
            s1[chunk, r] = jnp.concatenate(rows, axis=0).astype(bf16)
            return 0

        lax.fori_loop(0, LON, pack_residue, 0)
        if chunk == 0:
            pl.semaphore_wait(barrier, LON - 1 + 7 + 3)
            pl.semaphore_signal(ready, inc=1, device_id=partner, device_id_type=MESH)
        exchange(0, chunk)

    halo_down = pltpu.make_async_remote_copy(
        src_ref=cycles.at[ROWS], dst_ref=cycles.at[0], send_sem=halo_send.at[2],
        recv_sem=halo_recv.at[2], device_id=((lat + 1) % LAT, lon), device_id_type=MESH,
    )
    halo_up = pltpu.make_async_remote_copy(
        src_ref=cycles.at[1], dst_ref=cycles.at[ROWS + 1], send_sem=halo_send.at[3],
        recv_sem=halo_recv.at[3], device_id=((lat + LAT - 1) % LAT, lon), device_id_type=MESH,
    )
    halo_down.start()
    halo_up.start()

    for copy in fetches[1:]:
        copy.wait()
    making = legendre_orders(
        bin_index, owner, cycle_rows, log_norm, up_table, down_table, table, legendre
    )
    next(making)
    turned = pltpu.roll(gain[...], 64, axis=1)
    lane_half = lax.broadcasted_iota(jnp.int32, (M, HALF), 1) // 64
    gains[...] = jnp.where(lane_half == hemi, gain[...], turned)

    for chunk in range(3):
        far[...] = arrived(0, chunk)
        block = jnp.concatenate(
            [far[pl.ds(n, 32, stride=16), :] for n in range(16)], axis=1
        ).astype(bf16)
        result = dot(one[...], twice(block))
        for n in range(16):
            half, row = divmod(n, 8)
            lanes = slice(n * HALF, (n + 1) * HALF)
            quarters = trade(result[0:16, lanes], result[16:32, lanes])
            for g in range(2):
                near[pl.ds((g * LON + half) * 8 + row, 16, stride=16), :] = quarters[g]
        s2[chunk] = near[...].reshape(2 * LON, 8, HALF).astype(bf16)
        if chunk == 0:
            pl.semaphore_wait(ready, 1)
        exchange(1, chunk)

    next(making)

    halo_down.wait_recv()
    halo_up.wait_recv()
    edge = jnp.full((COLS, 2 * HALF), lat, jnp.int32)
    cycles[0] = jnp.where(edge > 0, cycles[0].astype(f32), 0.0).astype(bf16)
    cycles[ROWS + 1] = jnp.where(edge < LAT - 1, cycles[ROWS + 1].astype(f32), 0.0).astype(bf16)

    def pack_edges(y, _):
        row = cycles[y].astype(f32)
        edge_out[0, y] = row[COLS - SMAX :].astype(bf16)
        edge_out[1, y] = row[:SMAX].astype(bf16)
        return 0

    lax.fori_loop(0, ROWS + 2, pack_edges, 0)
    halo_right = pltpu.make_async_remote_copy(
        src_ref=edge_out.at[0], dst_ref=edge_in.at[0],
        send_sem=halo_send.at[0], recv_sem=halo_recv.at[0],
        device_id=(lat, (lon + 1) % LON), device_id_type=MESH,
    )
    halo_left = pltpu.make_async_remote_copy(
        src_ref=edge_out.at[1], dst_ref=edge_in.at[1],
        send_sem=halo_send.at[1], recv_sem=halo_recv.at[1],
        device_id=(lat, (lon + LON - 1) % LON), device_id_type=MESH,
    )

    for chunk in range(3):
        far[...] = arrived(1, chunk)
        if chunk == 2:
            halo_right.start()
            halo_left.start()
        columns = [
            jnp.concatenate(
                trade(far[pl.ds(row, 32, stride=8), :], far[pl.ds(256 + row, 32, stride=8), :]),
                axis=0,
            )
            for row in range(8)
        ]
        result = dot(two[...], twice(jnp.concatenate(columns, axis=1).astype(bf16)))
        for row in range(8):
            scaled = result[:, row * HALF : (row + 1) * HALF] * weight[pl.ds(chunk * 8 + row, 1), :]
            sides = trade(scaled[0:32], scaled[32:64])
            for g in range(2):
                for slot in range(4):
                    near[pl.ds(slot * 16 + g * 8 + row, 8, stride=64), :] = sides[g][
                        slot * 8 : slot * 8 + 8
                    ]
        s3[chunk] = near[...].reshape(8, 64, HALF).astype(bf16)
        exchange(2, chunk)

    for chunk in range(3):
        whole(2, chunk).wait_recv()
        lanes = slice(chunk * HALF, (chunk + 1) * HALF)
        for slot in range(4):
            data = g3[chunk, :, slot * 16 : slot * 16 + 16, :].reshape(HALF, HALF)
            part = dot(legendre[slot, :, lanes], data)
            if chunk == 0:
                total[slot] = part
            elif chunk == 1:
                total[slot] += part
            else:
                pooled[pl.ds(0, M), pl.ds(slot * HALF, HALF)] = (
                    (total[slot] + part) * gains[...]
                ).astype(bf16)
    for chunk in range(3):
        lanes = slice(chunk * HALF, (chunk + 1) * HALF)
        for slot in range(4):
            synthesis = lax.dot_general(
                legendre[slot, :, lanes],
                pooled[pl.ds(0, M), pl.ds(slot * HALF, HALF)],
                (((0,), (0,)), ((), ())),
                preferred_element_type=f32,
            )
            s4[chunk, :, slot * 16 : slot * 16 + 16, :] = synthesis.reshape(8, 16, HALF).astype(bf16)
        exchange(3, chunk)

    for chunk in range(3):
        far[...] = arrived(3, chunk)
        columns = []
        for row in range(8):
            sides = [
                jnp.concatenate(
                    [far[pl.ds(slot * 16 + g * 8 + row, 8, stride=64), :] for slot in range(4)],
                    axis=0,
                )
                for g in range(2)
            ]
            columns.append(jnp.concatenate(trade(*sides), axis=0))
        result = dot(three[...], twice(jnp.concatenate(columns, axis=1).astype(bf16)))
        for row in range(8):
            lanes = slice(row * HALF, (row + 1) * HALF)
            sides = trade(result[0:32, lanes], result[32:64, lanes])
            for g in range(2):
                near[pl.ds(g * 256 + row, 32, stride=8), :] = sides[g]
        s5[chunk] = near[...].reshape(2 * LON, 8, HALF).astype(bf16)
        exchange(4, chunk)

    halo_right.wait_recv()
    halo_left.wait_recv()

    def widen(y, _):
        sides = [edge_in[0, y], cycles[y], edge_in[1, y]]
        wide[y] = jnp.concatenate([side.astype(f32) for side in sides], axis=0).astype(bf16)
        return 0

    lax.fori_loop(0, ROWS + 2, widen, 0)
    source = lax.broadcasted_iota(jnp.int32, (COLS, COLS + 2 * SMAX), 1)
    target = lax.broadcasted_iota(jnp.int32, (COLS, COLS + 2 * SMAX), 0)
    offset = source - target - SMAX
    offset_real = offset.astype(f32)
    distance = jnp.abs(offset)
    distance_real = distance.astype(f32)

    def pool(y, _):
        half_width = jnp.full((COLS, COLS + 2 * SMAX), support[y], jnp.int32)
        span_len = (half_width + 1).astype(f32)
        inside = distance <= half_width
        triangle = jnp.where(inside, (span_len - distance_real) / span_len, 0.0)
        odd_basis = offset_real * triangle / span_len
        box_basis = jnp.where(inside, 1.0, 0.0) / jnp.sqrt(2.0 * half_width.astype(f32) + 1.0)
        band = jnp.concatenate([triangle, odd_basis, box_basis], axis=0).astype(bf16)
        start = pl.multiple_of(y * COLS, COLS)
        for a in range(3):
            basis = dot(band, wide[y + a]).astype(bf16)
            for k in range(3):
                pooled[pl.ds(start, COLS), pl.ds((a * 3 + k) * 256, 256)] = basis[
                    k * COLS : (k + 1) * COLS
                ]
        return 0

    lax.fori_loop(0, ROWS, pool, 0)

    for chunk in range(3):
        far[...] = arrived(4, chunk)
        columns = [
            jnp.concatenate(
                trade(far[pl.ds(n, 16, stride=16), :], far[pl.ds(256 + n, 16, stride=16), :]), axis=0
            )
            for n in range(16)
        ]
        result = dot(four[...], twice(jnp.concatenate(columns, axis=1).astype(bf16)))
        for n in range(16):
            near[pl.ds(n, 32, stride=16), :] = result[:, n * HALF : (n + 1) * HALF]
        s6[chunk] = near[...].reshape(LON, 16, HALF).astype(bf16)
        exchange(5, chunk)

    rows = ROWS * COLS // 4
    for part in range(4):
        convolved[part * rows : (part + 1) * rows, :] = dot(
            pooled[part * rows : (part + 1) * rows, :], conv_weight[...]
        )

    for chunk in range(3):
        far[...] = arrived(5, chunk)
        for row in range(8 if chunk < 2 else 7):
            y = chunk * 8 + row
            spectral = jnp.concatenate(
                [far[pl.ds(half * 8 + row, 32, stride=16), :] for half in range(2)], axis=1
            )
            branch = convolved[pl.ds(y * COLS, COLS), :] + spectral
            gelu = 0.5 * branch * (1.0 + lax.erf(branch * math.sqrt(0.5)))
            out[y] = (cycles[y + 1].astype(f32) + gelu).astype(bf16)

    for stage in range(6):
        for chunk in range(3):
            whole(stage, chunk).wait_send()
    for copy in (halo_right, halo_left, halo_down, halo_up):
        copy.wait_send()


def per_device(fields, conv_weight, spectral_gain, support):
    vmem = pl.BlockSpec(memory_space=pltpu.VMEM)
    hbm = pl.BlockSpec(memory_space=pltpu.HBM)
    f32, bf16 = jnp.float32, jnp.bfloat16
    by_ring = pltpu.VMEM((3, LON, 16, HALF), bf16)
    by_double = pltpu.VMEM((3, 2 * LON, 8, HALF), bf16)
    by_owner = pltpu.VMEM((3, 8, 64, HALF), bf16)
    tables = longitude_tables() + cycle_tables()
    return pl.pallas_call(
        block_kernel,
        out_shape=jax.ShapeDtypeStruct(fields.shape, fields.dtype),
        in_specs=[hbm] * 11,
        out_specs=vmem,
        scratch_shapes=[by_ring] * 2
        + [by_double] * 2
        + [by_owner] * 4
        + [by_double] * 2
        + [by_ring] * 2
        + [
            pltpu.VMEM((ROWS + 2, COLS + 2 * SMAX, 256), bf16),
            pltpu.VMEM((2, ROWS + 2, SMAX, 256), bf16),
            pltpu.VMEM((2, ROWS + 2, SMAX, 256), bf16),
            pltpu.VMEM((ROWS * COLS, 9 * 256), bf16),
            pltpu.VMEM((ROWS * COLS, 256), f32),
            pltpu.VMEM((512, HALF), f32),
            pltpu.VMEM((512, HALF), f32),
            pltpu.VMEM((2, PAD * COLS, HALF), f32),
            pltpu.VMEM((4 * M, HALF), f32),
            pltpu.VMEM((4 * M, HALF), f32),
            pltpu.VMEM((X // HALF, 4 * M, HALF), f32),
            pltpu.VMEM((4, M, X), bf16),
            pltpu.VMEM((M, HALF), f32),
            pltpu.VMEM((4, M, HALF), f32),
            pltpu.VMEM((ROWS + 2, COLS, 256), bf16),
            pltpu.VMEM((9 * 256, 256), bf16),
            pltpu.VMEM((M, HALF), f32),
            pltpu.SMEM((ROWS,), jnp.int32),
            pltpu.VMEM((32, 64), bf16),
            pltpu.VMEM((64, 128), bf16),
            pltpu.VMEM((64, 128), bf16),
            pltpu.VMEM((32, 64), bf16),
            pltpu.VMEM((3, X), f32),
            pltpu.VMEM((PAD, HALF), f32),
            pltpu.VMEM((1, M), f32),
            pltpu.SemaphoreType.DMA((11,)),
            pltpu.SemaphoreType.DMA((6, 3)),
            pltpu.SemaphoreType.DMA((6, 3)),
            pltpu.SemaphoreType.DMA((4,)),
            pltpu.SemaphoreType.DMA((4,)),
            pltpu.SemaphoreType.REGULAR,
        ],
        compiler_params=pltpu.CompilerParams(
            collective_id=0, has_side_effects=True, vmem_limit_bytes=64 * 2**20
        ),
    )(
        fields, conv_weight.reshape(9 * 256, 256), spectral_gain, support,
        *[jnp.asarray(table) for table in tables],
    )


def solution(mesh):
    placed = (P("lat", "lon", None), P(), P(), P("lat"))
    return jax.shard_map(
        per_device, mesh=mesh, in_specs=placed, out_specs=P("lat", "lon", None), check_vma=False
    )
```

```python
import functools
import math

import jax
import jax.numpy as jnp
import numpy as np
from jax import lax
from jax.experimental import pallas as pl
from jax.experimental.pallas import tpu as pltpu
from jax.sharding import PartitionSpec as P

NLAT = 368
NLON = 1024
M = 512
SMAX = 24
LAT = 16
LON = 32
ROWS = 23
PAD = 24
COLS = 32
HALF = 128
X = LAT * PAD
MESH = pl.DeviceIdType.MESH


def split_pair(table):
    upper_part = table.astype(jnp.bfloat16)
    lower_part = (table - upper_part.astype(jnp.float32)).astype(jnp.bfloat16)
    return upper_part, lower_part


def doubled(table):
    upper = table.astype(jnp.bfloat16)
    lower = (table - upper.astype(np.float32)).astype(jnp.bfloat16)
    return np.concatenate([upper, lower], axis=-1)


def orders_of(bin_index, lat_index):
    first = bin_index + 32 * lat_index
    second = (496 if bin_index == 0 else 512) - first
    return first, second


@functools.lru_cache
def longitude_tables():
    turn = 2.0 * np.pi / NLON
    b = np.arange(32)
    step_one = np.zeros((2, 16, 32))
    for q in range(16):
        step_one[0, q] = np.cos(2 * np.pi * b * q / 32)
        step_one[1, q] = np.sin(2 * np.pi * b * q / 32) if q else (-1.0) ** b
    step_one = step_one.reshape(32, 32)
    r = np.arange(32)
    step_two = np.zeros((16, 2, 2, 16, 2, 32))
    weight = np.zeros((16, 2, 2, 16))
    for q in range(16):
        for a in range(16):
            for u, m in enumerate(orders_of(q, a)):
                cos, sin = np.cos(turn * ((m * r) % NLON)), np.sin(turn * ((m * r) % NLON))
                weight[q, u, :, a] = 1.0 if m == 0 else 2.0
                if q == 0:
                    step_two[q, u, 0, a, u] = cos
                    step_two[q, u, 1, a, u] = sin
                else:
                    sign = 1.0 if u == 0 else -1.0
                    step_two[q, u, 0, a, 0] = cos
                    step_two[q, u, 0, a, 1] = -sign * sin
                    step_two[q, u, 1, a, 0] = sin
                    step_two[q, u, 1, a, 1] = sign * cos
    step_two = step_two.reshape(16, 2, 2, 8, 2, 64).transpose(0, 2, 4, 1, 3, 5).reshape(16, 64, 64)
    weight = weight.reshape(16, 2, 2, 8, 2).transpose(0, 2, 4, 1, 3).reshape(16, 64, 1)
    back = np.swapaxes(step_two * weight, 1, 2)
    f32 = np.float32
    return (
        doubled(step_one.astype(f32)),
        doubled((step_two / NLON).astype(f32)),
        doubled(back.astype(f32)),
        doubled(step_one.T.astype(f32)),
    )


@functools.lru_cache
def cycle_tables():
    t = np.pi * (np.arange(NLAT) + 0.5) / NLAT
    f32 = np.float32

    def placed(values):
        padded = np.zeros((LAT, PAD))
        padded[:, :ROWS] = values.reshape(LAT, ROWS)
        return padded.reshape(4, 2, 2, 3, 8).transpose(3, 0, 2, 1, 4).astype(f32)

    weight = placed(np.sin(t) * np.pi / NLAT).reshape(3, 8, 2, 8).transpose(1, 0, 3, 2)
    weight = np.repeat(weight.reshape(8, PAD, 2), 64, axis=2)
    k = np.arange(1, M)
    log_norm = np.concatenate([[0.0], np.cumsum(np.log((2 * k - 1) / (2 * k)))])
    log_norm = 0.5 * np.log((2 * np.arange(M) + 1) / 2) + 0.5 * log_norm
    rows = np.stack(
        [placed(np.cos(t)).reshape(X), placed(np.log(np.sin(t))).reshape(X), placed(np.ones(NLAT)).reshape(X)]
    )
    return rows, weight, log_norm.reshape(1, M).astype(f32)


def dot(left, right):
    return jnp.dot(left, right, preferred_element_type=jnp.float32)


def twice(block):
    return jnp.concatenate([block, block], axis=0)


def trade(first, second):
    low = lax.broadcasted_iota(jnp.int32, first.shape, 1) < 64
    return (
        jnp.where(low, first, pltpu.roll(second, 64, axis=1)),
        jnp.where(low, pltpu.roll(first, 64, axis=1), second),
    )


def legendre_orders(bin_index, owner, cycle_rows, log_norm, up_table, down_table, table, legendre):
    f32 = jnp.float32

    def order_rows(slot):
        first = bin_index + 64 * owner + 32 * (slot // 2)
        return jnp.where(slot % 2 == 0, first, jnp.where(bin_index == 0, 496, 512) - first)

    def coefficients(block, _):
        row = lax.broadcasted_iota(jnp.int32, (128, HALF), 0)
        degree = (block * 32 + row // 4).astype(f32)
        order = order_rows(row % 4).astype(f32)
        gap, total = degree - order, degree + order
        inside = gap > 0.5
        odd = 2.0 * degree + 1.0
        shared = odd / jnp.where(inside, gap * total, 1.0)
        rise = jnp.sqrt(shared * jnp.maximum(2.0 * degree - 1.0, 0.0))
        fall = jnp.sqrt(
            shared * jnp.maximum((gap - 1.0) * (total - 1.0), 0.0) / jnp.maximum(2.0 * degree - 3.0, 1.0)
        )
        start = pl.multiple_of(block * 128, 128)
        up_table[pl.ds(start, 128), :] = jnp.where(inside, rise, 0.0)
        down_table[pl.ds(start, 128), :] = jnp.where(inside, fall, 0.0)
        return 0

    lax.fori_loop(0, 16, coefficients, 0)
    order = order_rows(lax.broadcasted_iota(jnp.int32, (4, X), 0))
    wide_order = order_rows(lax.broadcasted_iota(jnp.int32, (4, M), 0))
    column = lax.broadcasted_iota(jnp.int32, (4, M), 1)
    norm = jnp.sum(jnp.where(column == wide_order, log_norm[...], 0.0), axis=1, keepdims=True)
    cosines = jnp.broadcast_to(cycle_rows[pl.ds(0, 1), :], (4, X))
    log_start = norm + order.astype(f32) * cycle_rows[pl.ds(1, 1), :]
    start_scale = jnp.minimum(log_start, 0.0)
    diagonal = jnp.exp(log_start - start_scale) * cycle_rows[pl.ds(2, 1), :]

    def spread(rows):
        return jnp.concatenate([rows] * (X // HALF), axis=1)

    def steps(block, state):
        latest, before, log_scale = state
        factor = jnp.exp(log_scale)
        for k in range(4):
            degree = block * 4 + k
            up = spread(up_table[pl.ds(4 * degree, 4), :]) * cosines
            down = spread(down_table[pl.ds(4 * degree, 4), :])
            current = up * latest + (jnp.where(order == degree, diagonal, 0.0) - down * before)
            value = current * factor
            for lane in range(X // HALF):
                table[lane, pl.ds(4 * degree, 4), :] = value[:, lane * HALF : (lane + 1) * HALF]
            latest, before = current, latest
        too_big = jnp.abs(latest) > 2.0**24
        shrink = jnp.where(too_big, 2.0**-24, 1.0)
        log_scale = jnp.where(too_big, log_scale + 24.0 * math.log(2.0), log_scale)
        return latest * shrink, before * shrink, log_scale

    blank = jnp.zeros((4, X), f32)
    state = lax.fori_loop(0, M // 8, steps, (blank, blank, start_scale))
    yield
    lax.fori_loop(M // 8, M // 4, steps, state)
    for slot in range(4):
        for lane in range(X // HALF):
            legendre[slot, :, lane * HALF : (lane + 1) * HALF] = table[
                lane, pl.ds(slot, M, stride=4), :
            ].astype(jnp.bfloat16)
    yield


def block_kernel(
    fields_in, conv_in, gain_in, support_in, one_in, two_in, three_in, four_in, cycles_in,
    weight_in, norm_in,
    out,
    s1, g1, s2, g2, s3, g3, s4, g4, s5, g5, s6, g6, wide, edge_out, edge_in, pooled, convolved,
    near, far, plain,
    up_table, down_table, table, legendre, gains, total,
    cycles, conv_weight, gain, support, one, two, three, four, cycle_rows, weight, log_norm,
    fetch, send, recv, halo_send, halo_recv, ready,
):
    lat = lax.axis_index("lat")
    lon = lax.axis_index("lon")
    hemi = lat // 2 % 2
    owner = lat // 4 * 2 + lat % 2
    spot = hemi * LON + lon
    double_base = lat // 4 * 4 + lat % 2
    bin_index, half_index = lon // 2, lon % 2
    f32, bf16 = jnp.float32, jnp.bfloat16

    own_lanes = pl.ds(pl.multiple_of(half_index * HALF, HALF), HALF)
    sources = [
        (fields_in, cycles.at[pl.ds(1, ROWS)]), (cycles_in, cycle_rows), (norm_in, log_norm), (one_in, one),
        (gain_in.at[:, own_lanes], gain), (two_in.at[bin_index], two),
        (weight_in.at[owner], weight), (three_in.at[bin_index], three), (support_in, support),
        (four_in, four), (conv_in, conv_weight),
    ]
    fetches = [
        pltpu.make_async_copy(source, target, fetch.at[index])
        for index, (source, target) in enumerate(sources)
    ]
    fetches[0].start()

    def double_peer(step):
        index = lax.rem(spot + step, 2 * LON)
        return index, (double_base + lax.div(index, LON) * 2, lax.rem(index, LON))

    def owner_peer(step):
        index = lax.rem(owner + step, 8)
        return index, (lax.div(index, 2) * 4 + hemi * 2 + lax.rem(index, 2), lon)

    def ring_peer(step):
        index = lax.rem(lon + step, LON)
        return index, (lat, index)

    barrier = pltpu.get_barrier_semaphore()

    def greet(peer_of):
        def one_peer(step, _):
            pl.semaphore_signal(barrier, inc=1, device_id=peer_of(step)[1], device_id_type=MESH)
            return 0

        return one_peer

    partner = (lat // 4 * 4 + (1 - hemi) * 2 + lat % 2, lon)
    lax.fori_loop(1, LON, greet(ring_peer), 0)
    lax.fori_loop(1, 8, greet(owner_peer), 0)
    for device in (((lat + 1) % LAT, lon), ((lat + LAT - 1) % LAT, lon), partner):
        pl.semaphore_signal(barrier, inc=1, device_id=device, device_id_type=MESH)
    for copy in fetches[1:]:
        copy.start()

    ring = (ring_peer, lon, LON)
    double = (double_peer, spot, 2 * LON)
    owners = (owner_peer, owner, 8)
    plan = [
        (s1, g1, ring), (s2, g2, double), (s3, g3, owners),
        (s4, g4, owners), (s5, g5, double), (s6, g6, ring),
    ]

    def exchange(stage, chunk):
        source, target, (peer_of, mine, count) = plan[stage]

        def one_peer(step):
            peer, device = peer_of(step)
            pltpu.make_async_remote_copy(
                src_ref=source.at[chunk, peer], dst_ref=target.at[chunk, mine],
                send_sem=send.at[stage, chunk], recv_sem=recv.at[stage, chunk],
                device_id=device, device_id_type=MESH,
            ).start()

        def three_peers(turn, _):
            for k in range(3):
                one_peer(turn * 3 + 1 + k)
            return 0

        lax.fori_loop(0, (count - 1) // 3, three_peers, 0)
        if (count - 1) % 3:
            one_peer(count - 1)
        target[chunk, mine] = source[chunk, mine]

    def whole(stage, chunk):
        source, target, (_, _, count) = plan[stage]
        return pltpu.make_async_remote_copy(
            src_ref=source.at[chunk, pl.ds(0, count - 1)],
            dst_ref=target.at[chunk, pl.ds(0, count - 1)],
            send_sem=send.at[stage, chunk], recv_sem=recv.at[stage, chunk],
            device_id=(lat, (lon + 1) % LON), device_id_type=MESH,
        )

    def arrived(stage, chunk):
        whole(stage, chunk).wait_recv()
        target = plan[stage][1]
        return target[chunk].astype(f32).reshape(512, HALF)

    fetches[0].wait()
    for chunk in range(3):
        count = min(8, ROWS - chunk * 8)
        for half in range(2):
            lanes = slice(half * HALF, (half + 1) * HALF)
            plain[half, pl.ds(chunk * 8 * COLS, count * COLS), :] = (
                cycles[chunk * 8 + 1 : chunk * 8 + 1 + count, :, lanes]
                .astype(f32)
                .reshape(count * COLS, HALF)
            )
            if count < 8:
                plain[half, pl.ds(ROWS * COLS, COLS), :] = jnp.zeros((COLS, HALF), f32)

        def pack_residue(r, _, chunk=chunk):
            rows = [
                plain[half, pl.ds(chunk * 8 * COLS + r, 8, stride=COLS), :] for half in range(2)
            ]
            s1[chunk, r] = jnp.concatenate(rows, axis=0).astype(bf16)
            return 0

        lax.fori_loop(0, LON, pack_residue, 0)
        if chunk == 0:
            pl.semaphore_wait(barrier, LON - 1 + 7 + 3)
            pl.semaphore_signal(ready, inc=1, device_id=partner, device_id_type=MESH)
        exchange(0, chunk)

    halo_down = pltpu.make_async_remote_copy(
        src_ref=cycles.at[ROWS], dst_ref=cycles.at[0], send_sem=halo_send.at[2],
        recv_sem=halo_recv.at[2], device_id=((lat + 1) % LAT, lon), device_id_type=MESH,
    )
    halo_up = pltpu.make_async_remote_copy(
        src_ref=cycles.at[1], dst_ref=cycles.at[ROWS + 1], send_sem=halo_send.at[3],
        recv_sem=halo_recv.at[3], device_id=((lat + LAT - 1) % LAT, lon), device_id_type=MESH,
    )
    halo_down.start()
    halo_up.start()

    for copy in fetches[1:]:
        copy.wait()
    making = legendre_orders(
        bin_index, owner, cycle_rows, log_norm, up_table, down_table, table, legendre
    )
    next(making)
    turned = pltpu.roll(gain[...], 64, axis=1)
    lane_half = lax.broadcasted_iota(jnp.int32, (M, HALF), 1) // 64
    gains[...] = jnp.where(lane_half == hemi, gain[...], turned)

    for chunk in range(3):
        far[...] = arrived(0, chunk)
        block = jnp.concatenate(
            [far[pl.ds(n, 32, stride=16), :] for n in range(16)], axis=1
        ).astype(bf16)
        result = dot(one[...], twice(block))
        for n in range(16):
            half, row = divmod(n, 8)
            lanes = slice(n * HALF, (n + 1) * HALF)
            quarters = trade(result[0:16, lanes], result[16:32, lanes])
            for g in range(2):
                near[pl.ds((g * LON + half) * 8 + row, 16, stride=16), :] = quarters[g]
        s2[chunk] = near[...].reshape(2 * LON, 8, HALF).astype(bf16)
        if chunk == 0:
            pl.semaphore_wait(ready, 1)
        exchange(1, chunk)

    next(making)

    halo_down.wait_recv()
    halo_up.wait_recv()
    edge = jnp.full((COLS, 2 * HALF), lat, jnp.int32)
    cycles[0] = jnp.where(edge > 0, cycles[0].astype(f32), 0.0).astype(bf16)
    cycles[ROWS + 1] = jnp.where(edge < LAT - 1, cycles[ROWS + 1].astype(f32), 0.0).astype(bf16)

    def pack_edges(y, _):
        row = cycles[y].astype(f32)
        edge_out[0, y] = row[COLS - SMAX :].astype(bf16)
        edge_out[1, y] = row[:SMAX].astype(bf16)
        return 0

    lax.fori_loop(0, ROWS + 2, pack_edges, 0)
    halo_right = pltpu.make_async_remote_copy(
        src_ref=edge_out.at[0], dst_ref=edge_in.at[0],
        send_sem=halo_send.at[0], recv_sem=halo_recv.at[0],
        device_id=(lat, (lon + 1) % LON), device_id_type=MESH,
    )
    halo_left = pltpu.make_async_remote_copy(
        src_ref=edge_out.at[1], dst_ref=edge_in.at[1],
        send_sem=halo_send.at[1], recv_sem=halo_recv.at[1],
        device_id=(lat, (lon + LON - 1) % LON), device_id_type=MESH,
    )

    for chunk in range(3):
        far[...] = arrived(1, chunk)
        if chunk == 2:
            halo_right.start()
            halo_left.start()
        columns = [
            jnp.concatenate(
                trade(far[pl.ds(row, 32, stride=8), :], far[pl.ds(256 + row, 32, stride=8), :]),
                axis=0,
            )
            for row in range(8)
        ]
        result = dot(two[...], twice(jnp.concatenate(columns, axis=1).astype(bf16)))
        for row in range(8):
            scaled = result[:, row * HALF : (row + 1) * HALF] * weight[pl.ds(chunk * 8 + row, 1), :]
            sides = trade(scaled[0:32], scaled[32:64])
            for g in range(2):
                for slot in range(4):
                    near[pl.ds(slot * 16 + g * 8 + row, 8, stride=64), :] = sides[g][
                        slot * 8 : slot * 8 + 8
                    ]
        s3[chunk] = near[...].reshape(8, 64, HALF).astype(bf16)
        exchange(2, chunk)

    for chunk in range(3):
        whole(2, chunk).wait_recv()
        lanes = slice(chunk * HALF, (chunk + 1) * HALF)
        for slot in range(4):
            data = g3[chunk, :, slot * 16 : slot * 16 + 16, :].reshape(HALF, HALF)
            part = dot(legendre[slot, :, lanes], data)
            if chunk == 0:
                total[slot] = part
            elif chunk == 1:
                total[slot] += part
            else:
                pooled[pl.ds(0, M), pl.ds(slot * HALF, HALF)] = (
                    (total[slot] + part) * gains[...]
                ).astype(bf16)
    for chunk in range(3):
        lanes = slice(chunk * HALF, (chunk + 1) * HALF)
        for slot in range(4):
            synthesis = lax.dot_general(
                legendre[slot, :, lanes],
                pooled[pl.ds(0, M), pl.ds(slot * HALF, HALF)],
                (((0,), (0,)), ((), ())),
                preferred_element_type=f32,
            )
            s4[chunk, :, slot * 16 : slot * 16 + 16, :] = synthesis.reshape(8, 16, HALF).astype(bf16)
        exchange(3, chunk)

    for chunk in range(3):
        far[...] = arrived(3, chunk)
        columns = []
        for row in range(8):
            sides = [
                jnp.concatenate(
                    [far[pl.ds(slot * 16 + g * 8 + row, 8, stride=64), :] for slot in range(4)],
                    axis=0,
                )
                for g in range(2)
            ]
            columns.append(jnp.concatenate(trade(*sides), axis=0))
        result = dot(three[...], twice(jnp.concatenate(columns, axis=1).astype(bf16)))
        for row in range(8):
            lanes = slice(row * HALF, (row + 1) * HALF)
            sides = trade(result[0:32, lanes], result[32:64, lanes])
            for g in range(2):
                near[pl.ds(g * 256 + row, 32, stride=8), :] = sides[g]
        s5[chunk] = near[...].reshape(2 * LON, 8, HALF).astype(bf16)
        exchange(4, chunk)

    halo_right.wait_recv()
    halo_left.wait_recv()

    def widen(y, _):
        sides = [edge_in[0, y], cycles[y], edge_in[1, y]]
        wide[y] = jnp.concatenate([side.astype(f32) for side in sides], axis=0).astype(bf16)
        return 0

    lax.fori_loop(0, ROWS + 2, widen, 0)
    source = lax.broadcasted_iota(jnp.int32, (COLS, COLS + 2 * SMAX), 1)
    target = lax.broadcasted_iota(jnp.int32, (COLS, COLS + 2 * SMAX), 0)
    offset = source - target - SMAX
    offset_real = offset.astype(f32)
    distance = jnp.abs(offset)
    distance_real = distance.astype(f32)

    def pool(y, _):
        half_width = jnp.full((COLS, COLS + 2 * SMAX), support[y], jnp.int32)
        span_len = (half_width + 1).astype(f32)
        inside = distance <= half_width
        triangle = jnp.where(inside, (span_len - distance_real) / span_len, 0.0)
        odd_basis = offset_real * triangle / span_len
        box_basis = jnp.where(inside, 1.0, 0.0) / jnp.sqrt(2.0 * half_width.astype(f32) + 1.0)
        band = jnp.concatenate([triangle, odd_basis, box_basis], axis=0).astype(bf16)
        start = pl.multiple_of(y * COLS, COLS)
        for a in range(3):
            basis = dot(band, wide[y + a]).astype(bf16)
            for k in range(3):
                pooled[pl.ds(start, COLS), pl.ds((a * 3 + k) * 256, 256)] = basis[
                    k * COLS : (k + 1) * COLS
                ]
        return 0

    lax.fori_loop(0, ROWS, pool, 0)

    for chunk in range(3):
        far[...] = arrived(4, chunk)
        columns = [
            jnp.concatenate(
                trade(far[pl.ds(n, 16, stride=16), :], far[pl.ds(256 + n, 16, stride=16), :]), axis=0
            )
            for n in range(16)
        ]
        result = dot(four[...], twice(jnp.concatenate(columns, axis=1).astype(bf16)))
        for n in range(16):
            near[pl.ds(n, 32, stride=16), :] = result[:, n * HALF : (n + 1) * HALF]
        s6[chunk] = near[...].reshape(LON, 16, HALF).astype(bf16)
        exchange(5, chunk)

    rows = ROWS * COLS // 4
    for part in range(4):
        convolved[part * rows : (part + 1) * rows, :] = dot(
            pooled[part * rows : (part + 1) * rows, :], conv_weight[...]
        )

    for chunk in range(3):
        far[...] = arrived(5, chunk)
        for row in range(8 if chunk < 2 else 7):
            y = chunk * 8 + row
            spectral = jnp.concatenate(
                [far[pl.ds(half * 8 + row, 32, stride=16), :] for half in range(2)], axis=1
            )
            branch = convolved[pl.ds(y * COLS, COLS), :] + spectral
            gelu = 0.5 * branch * (1.0 + lax.erf(branch * math.sqrt(0.5)))
            out[y] = (cycles[y + 1].astype(f32) + gelu).astype(bf16)

    for stage in range(6):
        for chunk in range(3):
            whole(stage, chunk).wait_send()
    for copy in (halo_right, halo_left, halo_down, halo_up):
        copy.wait_send()


def per_device(fields, conv_weight, spectral_gain, support):
    vmem = pl.BlockSpec(memory_space=pltpu.VMEM)
    hbm = pl.BlockSpec(memory_space=pltpu.HBM)
    f32, bf16 = jnp.float32, jnp.bfloat16
    by_ring = pltpu.VMEM((3, LON, 16, HALF), bf16)
    by_double = pltpu.VMEM((3, 2 * LON, 8, HALF), bf16)
    by_owner = pltpu.VMEM((3, 8, 64, HALF), bf16)
    tables = longitude_tables() + cycle_tables()
    return pl.pallas_call(
        block_kernel,
        out_shape=jax.ShapeDtypeStruct(fields.shape, fields.dtype),
        in_specs=[hbm] * 11,
        out_specs=vmem,
        scratch_shapes=[by_ring] * 2
        + [by_double] * 2
        + [by_owner] * 4
        + [by_double] * 2
        + [by_ring] * 2
        + [
            pltpu.VMEM((ROWS + 2, COLS + 2 * SMAX, 256), bf16),
            pltpu.VMEM((2, ROWS + 2, SMAX, 256), bf16),
            pltpu.VMEM((2, ROWS + 2, SMAX, 256), bf16),
            pltpu.VMEM((ROWS * COLS, 9 * 256), bf16),
            pltpu.VMEM((ROWS * COLS, 256), f32),
            pltpu.VMEM((512, HALF), f32),
            pltpu.VMEM((512, HALF), f32),
            pltpu.VMEM((2, PAD * COLS, HALF), f32),
            pltpu.VMEM((4 * M, HALF), f32),
            pltpu.VMEM((4 * M, HALF), f32),
            pltpu.VMEM((X // HALF, 4 * M, HALF), f32),
            pltpu.VMEM((4, M, X), bf16),
            pltpu.VMEM((M, HALF), f32),
            pltpu.VMEM((4, M, HALF), f32),
            pltpu.VMEM((ROWS + 2, COLS, 256), bf16),
            pltpu.VMEM((9 * 256, 256), bf16),
            pltpu.VMEM((M, HALF), f32),
            pltpu.SMEM((ROWS,), jnp.int32),
            pltpu.VMEM((32, 64), bf16),
            pltpu.VMEM((64, 128), bf16),
            pltpu.VMEM((64, 128), bf16),
            pltpu.VMEM((32, 64), bf16),
            pltpu.VMEM((3, X), f32),
            pltpu.VMEM((PAD, HALF), f32),
            pltpu.VMEM((1, M), f32),
            pltpu.SemaphoreType.DMA((11,)),
            pltpu.SemaphoreType.DMA((6, 3)),
            pltpu.SemaphoreType.DMA((6, 3)),
            pltpu.SemaphoreType.DMA((4,)),
            pltpu.SemaphoreType.DMA((4,)),
            pltpu.SemaphoreType.REGULAR,
        ],
        compiler_params=pltpu.CompilerParams(
            collective_id=0, has_side_effects=True, vmem_limit_bytes=64 * 2**20
        ),
    )(
        fields, conv_weight.reshape(9 * 256, 256), spectral_gain, support,
        *[jnp.asarray(table) for table in tables],
    )


def solution(mesh):
    placed = (P("lat", "lon", None), P(), P(), P("lat"))
    return jax.shard_map(
        per_device, mesh=mesh, in_specs=placed, out_specs=P("lat", "lon", None), check_vma=False
    )
```
